32 devices in a mesh: grp: 1, ffn: 8 (over z, core), tok: 4 (over y, x).
Axes of the slice: x: 2, y: 2, z: 4, core: 2. Of those that a mesh axis runs over, the one named last changes fastest.
Arguments:
- tokens: bfloat16 [1024, 16384], P(('grp', 'tok'), 'ffn'), may hold values from -6 to 6
- gate_blocks: bfloat16 [1024, 53248], P(('grp', 'tok'), 'ffn'), may hold values from -0.1875 to 0.1875
- up_blocks: bfloat16 [1024, 53248], P(('grp', 'tok'), 'ffn'), may hold values from -0.1875 to 0.1875
- block_rows: int32 [416, 8], P(('grp', 'ffn')), may hold values from 0 to 127, all different within a row
- slab_offset: int32 [1], P('grp'), may hold values from 0 to 49152, as said below
Outputs:
- hessian_slab: float32 [4096, 53248], P(('grp', 'tok'), 'ffn')
The draws below stay inside these ranges and needn't reach their ends.
Inputs may be any that keep to these rules, and one draw needn't show every extreme that they name: `block_rows`: each row holds 8 different row-block numbers, and every row-block number appears somewhere. `slab_offset`: a multiple of 128.
All inputs are finite; a program needn't handle non-finite values.
Results may differ from the reference program's by a relative error of at most 0.004.
Values may be sent and summed in bfloat16 or wider, within the bound.
A program may use at most 192 MiB of HBM per device.

```python
import jax
import jax.numpy as jnp
from jax import lax

D = 16384
FF = 53248
BLOCK = 128
NNZ = 8
SLAB = 4096
TOKENS = 1024


def draw_slab_offset(key, part):
    key = jax.random.fold_in(key, 7)
    return (jax.random.randint(key, (1,), 0, (FF - SLAB) // BLOCK + 1) * BLOCK).astype(jnp.int32)


def steps_of(rng, dims, split, smallest, largest):
    factor_of = 1.0
    for dim, parts in split:
        steps = jax.random.uniform(jax.random.fold_in(jax.random.fold_in(rng, 6), dim), (parts,), jnp.float32, smallest / len(split), largest / len(split))
        factor_of = factor_of * jnp.repeat(jnp.exp(steps), dims[dim] // parts).reshape((-1,) + (1,) * (len(dims) - 1 - dim))
    return factor_of


def choose_distinct(rng, rows, amount, top, lift):
    sequence = jax.random.permutation(jax.random.fold_in(rng, 1), amount)
    boost = sequence
    for power in range(3):
        boost = boost * boost // amount
    boost = boost * lift // amount
    tickets = jax.random.randint(jax.random.fold_in(rng, 2), (rows, amount), 0, 4096) + boost
    sure = jax.random.permutation(jax.random.fold_in(rng, 3), rows)[jnp.arange(amount) % rows]
    tickets = jnp.where(jnp.arange(rows)[:, None] == sure[None, :], 1 << 14, tickets)
    merit = tickets * amount + jnp.arange(amount)
    return lax.top_k(merit.astype(jnp.int32), top)[1].astype(jnp.int32)


def normal_values(stream_key, dims, deviation, bound, cuts=(), held_as=jnp.bfloat16):
    entries = jax.random.normal(stream_key, dims, jnp.float32) * deviation
    if len(cuts) > 0:
        entries = steps_of(stream_key, dims, cuts, -0.22, 0.18) * entries
    return jnp.clip(entries, min=-bound, max=bound).astype(held_as)


def setup_inputs(seed: int = 0, part: int = 0) -> dict:
    key_list = jax.random.split(jax.random.key(seed), 6)
    own_keys = jax.random.split(jax.random.fold_in(key_list[5], part), 6)
    tokens = normal_values(own_keys[0], (TOKENS, D), 1.0, 6.0, ((0, 4), (1, 8)))
    gate_blocks = normal_values(own_keys[1], (NNZ * BLOCK, FF), (NNZ * BLOCK) ** -0.5, 0.1875, ((0, 4), (1, 8)))
    up_blocks = normal_values(own_keys[2], (NNZ * BLOCK, FF), (NNZ * BLOCK) ** -0.5, 0.1875, ((0, 4), (1, 8)))
    block_rows = choose_distinct(own_keys[3], (FF // BLOCK), D // BLOCK, NNZ, 0)
    slab_offset = draw_slab_offset(jax.random.fold_in(jax.random.fold_in(key_list[5], part), 71), part)
    return dict(tokens=tokens, gate_blocks=gate_blocks, up_blocks=up_blocks, block_rows=block_rows, slab_offset=slab_offset)


def reference(tokens, gate_blocks, up_blocks, block_rows, slab_offset):
    token_blocks = tokens.reshape(TOKENS, D // BLOCK, BLOCK)
    gate_tiles = gate_blocks.reshape(NNZ, BLOCK, FF // BLOCK, BLOCK).transpose(2, 0, 1, 3)
    up_tiles = up_blocks.reshape(NNZ, BLOCK, FF // BLOCK, BLOCK).transpose(2, 0, 1, 3)

    def column(inputs):
        row_ids, gate_tile, up_tile = inputs
        picked = jnp.take(token_blocks, row_ids, axis=1).astype(jnp.float32)
        gate_act = jnp.einsum('tkr,krs->ts', picked, gate_tile.astype(jnp.float32))
        up_act = jnp.einsum('tkr,krs->ts', picked, up_tile.astype(jnp.float32))
        return (jax.nn.silu(gate_act) * up_act).astype(jnp.bfloat16)

    hidden = lax.map(column, (block_rows, gate_tiles, up_tiles))
    hidden = hidden.transpose(1, 0, 2).reshape(TOKENS, FF)
    slab = lax.dynamic_slice_in_dim(hidden, slab_offset[0].astype(jnp.int32), SLAB, 1)
    hessian_segments = slab.reshape(TOKENS, SLAB // BLOCK, BLOCK).transpose(1, 0, 2)

    def slab_rows(part):
        return jnp.dot(part.T, hidden, preferred_element_type=jnp.float32) * (2.0 / TOKENS)

    result = lax.map(slab_rows, hessian_segments)
    return result.reshape(SLAB, FF)
```

```python
import functools

import jax
import jax.numpy as jnp
from jax import lax
from jax.experimental import pallas as pl
from jax.experimental.pallas import tpu as pltpu
from jax.sharding import PartitionSpec as P

BLOCK = 128
SLAB = 4096
MESH = pl.DeviceIdType.MESH
ANY = pl.BlockSpec(memory_space=pl.ANY)


def remote(src, dst, send, recv, **where):
    return pltpu.make_async_remote_copy(
        src_ref=src, dst_ref=dst, send_sem=send, recv_sem=recv, device_id=where, device_id_type=MESH
    )


def greet(others, z_there):
    barrier = pltpu.get_barrier_semaphore()
    for where in others:
        pl.semaphore_signal(barrier, inc=1, device_id=where, device_id_type=MESH)
    for there, where in z_there:
        @pl.when(there)
        def _():
            pl.semaphore_signal(barrier, inc=1, device_id=where, device_id_type=MESH)
    count = len(others)
    for there, _ in z_there:
        count = count + jnp.where(there, 1, 0)
    pl.semaphore_wait(barrier, count)


def places():
    f, t = lax.axis_index("ffn"), lax.axis_index("tok")
    z, c = f // 2, f % 2
    y, x = t // 2, t % 2
    return f, t, z, c, y, x


def spread(chips, tok_ref, gate_ref, up_ref, t_ref, g_ref, u_ref,
           w_send, w_recv, l_sem, x_send, x_recv, c_send, c_recv, up_send, up_recv, dn_send, dn_recv):
    f, t, z, c, y, x = places()
    half = g_ref.shape[2]
    xn, yn, dn = y * 2 + 1 - x, (1 - y) * 2 + x, (1 - y) * 2 + 1 - x
    partner = z * 2 + 1 - c
    above, below = f + 2, f - 2
    greet(
        [dict(tok=xn), dict(tok=yn), dict(tok=dn), dict(ffn=partner)],
        [(z < chips - 1, dict(ffn=above)), (z > 0, dict(ffn=below))],
    )
    ends = []
    own = t_ref.at[f, x]
    cx = remote(tok_ref, own, x_send, x_recv, tok=xn)
    cx.start()

    def up(src, dst, zs, j):
        return remote(src, dst, up_send.at[zs, j], up_recv.at[zs, j], ffn=above)

    def down(src, dst, zs, j):
        return remote(src, dst, dn_send.at[zs, j], dn_recv.at[zs, j], ffn=below)

    def across(src, dst, zs, j):
        return remote(src, dst, c_send.at[zs, j], c_recv.at[zs, j], ffn=partner)

    def pass_on(src, dst, zs, j, go_up, go_down):
        if go_up is not None:
            @pl.when(go_up)
            def _():
                up(src, dst, zs, j).start()
        if go_down is not None:
            @pl.when(go_down)
            def _():
                down(src, dst, zs, j).start()
        across(src, dst, zs, j).start()

    pass_on(tok_ref, own, z, 0, z < chips - 1, z > 0)
    copies = []
    for k, (there, x_there) in enumerate(((xn, 1 - x), (yn, x), (dn, 1 - x))):
        cols = pl.ds(pl.multiple_of(x_there * half, BLOCK), half)
        for m, (src, dst) in enumerate(((gate_ref, g_ref), (up_ref, u_ref))):
            copy = remote(src.at[:, cols], dst.at[t], w_send.at[k, m], w_recv.at[k, m], tok=there)
            copy.start()
            copies.append(copy)
    cols = pl.ds(pl.multiple_of(x * half, BLOCK), half)
    locals_ = [
        pltpu.make_async_copy(tok_ref, own, l_sem.at[0]),
        pltpu.make_async_copy(gate_ref.at[:, cols], g_ref.at[t], l_sem.at[1]),
        pltpu.make_async_copy(up_ref.at[:, cols], u_ref.at[t], l_sem.at[2]),
    ]
    for copy in locals_:
        copy.start()
    other = t_ref.at[f, 1 - x]
    remote(tok_ref, other, x_send, x_recv, tok=xn).wait_recv()
    pass_on(other, other, z, 1, z < chips - 1, z > 0)
    for k in range(1, chips):
        for j in range(2):
            xs = x if j == 0 else 1 - x

            @pl.when(z >= k)
            def _():
                piece = t_ref.at[f - 2 * k, xs]
                up(piece, piece, z - k, j).wait_recv()
                pass_on(piece, piece, z - k, j, z < chips - 1, None)

            @pl.when(z + k < chips)
            def _():
                piece = t_ref.at[f + 2 * k, xs]
                down(piece, piece, z + k, j).wait_recv()
                pass_on(piece, piece, z + k, j, None, z > 0)

    for zs in range(chips):
        for j in range(2):
            xs = x if j == 0 else 1 - x
            got = t_ref.at[zs * 2 + 1 - c, xs]
            across(got, got, zs, j).wait_recv()
            across(got, got, zs, j).wait_send()

            @pl.when((zs <= z) & (z < chips - 1))
            def _():
                up(got, got, zs, j).wait_send()

            @pl.when((zs >= z) & (z > 0))
            def _():
                down(got, got, zs, j).wait_send()

    cx.wait_send()
    for copy in locals_:
        copy.wait()
    for copy in copies:
        copy.wait()


def join(h_ref, p_ref, l_sem, send, recv):
    f, t, z, c, y, x = places()
    rows, half = h_ref.shape
    xn, yn, dn = y * 2 + 1 - x, (1 - y) * 2 + x, (1 - y) * 2 + 1 - x
    greet([dict(tok=xn), dict(tok=yn)], [])
    cut = rows // 2

    def part(yy, xx, s):
        return p_ref.at[
            pl.ds(pl.multiple_of(yy * rows + s * cut, 16), cut),
            pl.ds(pl.multiple_of(xx * half, BLOCK), half),
        ]

    local = pltpu.make_async_copy(
        h_ref,
        p_ref.at[pl.ds(pl.multiple_of(y * rows, 16), rows), pl.ds(pl.multiple_of(x * half, BLOCK), half)],
        l_sem,
    )

    def copy(src, yy, xx, s, n, there):
        return remote(src, part(yy, xx, s), send.at[n], recv.at[n], tok=there)

    own = [h_ref.at[pl.ds(s * cut, cut)] for s in range(2)]
    sent = [
        copy(own[0], y, x, 0, 0, xn), copy(own[1], y, x, 1, 2, yn),
        copy(own[1], y, x, 1, 1, xn), copy(own[0], y, x, 0, 3, yn),
    ]
    for s in sent:
        s.start()
    local.start()
    a = part(y, 1 - x, 0)
    copy(a, y, 1 - x, 0, 0, xn).wait_recv()
    fy = copy(a, y, 1 - x, 0, 4, yn)
    fy.start()
    b = part(1 - y, x, 1)
    copy(b, 1 - y, x, 1, 2, yn).wait_recv()
    fx = copy(b, 1 - y, x, 1, 5, xn)
    fx.start()
    sent[2].wait_recv()
    sent[3].wait_recv()
    fy.wait()
    fx.wait()
    for s in sent:
        s.wait_send()
    local.wait()


def hidden_kernel(per, rows_ref, t_ref, g_ref, u_ref, h_ref):
    i = pl.program_id(0)
    depth = g_ref.shape[0]
    tiles = []
    for k in range(depth // BLOCK):
        r = rows_ref[i, k]
        tile = t_ref[r // per, :, :, pl.ds(pl.multiple_of((r % per) * BLOCK, BLOCK), BLOCK)]
        tiles.append(tile.reshape(-1, BLOCK))
    picked = jnp.concatenate(tiles, axis=1)
    weights = jnp.concatenate([g_ref[...], u_ref[...]], axis=1)
    both = jnp.dot(picked, weights, preferred_element_type=jnp.float32)
    gate, up = both[:, :BLOCK], both[:, BLOCK:]
    h_ref[...] = (gate / (1.0 + jnp.exp(-gate)) * up).astype(h_ref.dtype)


def product_kernel(scale, a_ref, b_ref, o_ref):
    o_ref[...] = jnp.dot(a_ref[...], b_ref[...], preferred_element_type=jnp.float32) * scale


def params(**more):
    return pltpu.CompilerParams(**more)


def shards_split(ffn, tokens, gate_blocks, up_blocks, block_rows, slab_offset):
    rows, feats = tokens.shape
    depth, panel = gate_blocks.shape
    half = panel // 2
    chips = ffn // 2
    bf = jnp.bfloat16
    dma = pltpu.SemaphoreType.DMA
    shape = jax.ShapeDtypeStruct
    spread_tokens, gates, ups = pl.pallas_call(
        functools.partial(spread, chips),
        out_shape=(shape((ffn, 2, rows, feats), bf), shape((4, depth, half), bf), shape((4, depth, half), bf)),
        in_specs=[ANY] * 3,
        out_specs=(ANY,) * 3,
        scratch_shapes=[
            dma((3, 2)), dma((3, 2)), dma((3,)), dma, dma,
            dma((chips, 2)), dma((chips, 2)), dma((chips, 2)),
            dma((chips, 2)), dma((chips, 2)), dma((chips, 2)),
        ],
        compiler_params=params(collective_id=0, has_side_effects=True),
        name="spread",
    )(tokens, gate_blocks, up_blocks)
    t = lax.axis_index("tok")
    f = lax.axis_index("ffn")
    count = half // BLOCK
    rows_here = lax.dynamic_slice_in_dim(block_rows, (t % 2) * count, count, 0)
    hidden = pl.pallas_call(
        functools.partial(hidden_kernel, feats // BLOCK),
        out_shape=shape((2 * rows, half), bf),
        grid_spec=pltpu.PrefetchScalarGridSpec(
            num_scalar_prefetch=1,
            grid=(count,),
            in_specs=[
                pl.BlockSpec(memory_space=pltpu.VMEM),
                pl.BlockSpec((4 * depth, BLOCK), lambda i, r: (0, i)),
                pl.BlockSpec((4 * depth, BLOCK), lambda i, r: (0, i)),
            ],
            out_specs=pl.BlockSpec((2 * rows, BLOCK), lambda i, r: (0, i)),
        ),
        compiler_params=params(vmem_limit_bytes=48 * 1024 * 1024),
        name="hidden",
    )(rows_here, spread_tokens, gates.reshape(4 * depth, half), ups.reshape(4 * depth, half))
    whole = pl.pallas_call(
        join,
        out_shape=shape((4 * rows, panel), bf),
        in_specs=[ANY],
        out_specs=ANY,
        scratch_shapes=[dma, dma((6,)), dma((6,))],
        compiler_params=params(collective_id=1, has_side_effects=True),
        name="join",
    )(hidden)
    wide = SLAB // 4
    begin = slab_offset[0] + t * wide - f * panel
    padded = jnp.pad(whole, ((0, 0), (wide, wide)))
    piece = lax.dynamic_slice_in_dim(padded, jnp.clip(begin + wide, 0, panel + wide), wide, 1)
    row_panel = lax.psum(piece, "ffn").T
    tile = 512 if panel % 512 == 0 else BLOCK
    return pl.pallas_call(
        functools.partial(product_kernel, 2.0 / (4 * rows)),
        out_shape=shape((wide, panel), jnp.float32),
        grid=(panel // tile,),
        in_specs=[
            pl.BlockSpec((wide, 4 * rows), lambda i: (0, 0)),
            pl.BlockSpec((4 * rows, tile), lambda i: (0, i)),
        ],
        out_specs=pl.BlockSpec((wide, tile), lambda i: (0, i)),
        compiler_params=params(vmem_limit_bytes=48 * 1024 * 1024),
        name="product",
    )(row_panel, whole)


def shards(tokens, gate_blocks, up_blocks, block_rows, slab_offset):
    rows_here = tokens.shape[0]
    column_count = block_rows.shape[0]
    whole = lax.all_gather(tokens, "ffn", axis=1, tiled=True)
    feature_tiles = whole.reshape(rows_here, -1, BLOCK)
    chosen_entries = jnp.take(feature_tiles, block_rows, axis=1)
    pieces = (
        lax.all_gather(gate_blocks, "tok", axis=0, tiled=True),
        lax.all_gather(up_blocks, "tok", axis=0, tiled=True),
    )
    block_count = pieces[0].shape[0] // BLOCK
    gate_segment = pieces[0].reshape(block_count, BLOCK, column_count, BLOCK)
    up_segment = pieces[1].reshape(block_count, BLOCK, column_count, BLOCK)
    gate_add = jnp.einsum(
        "aqdh,dhqz->aqz", chosen_entries, gate_segment, preferred_element_type=jnp.float32
    )
    up_increment = jnp.einsum(
        "aqdh,dhqz->aqz", chosen_entries, up_segment, preferred_element_type=jnp.float32
    )
    panel_width = column_count * BLOCK
    hidden = (
        (jax.nn.silu(gate_add) * up_increment).astype(jnp.bfloat16).reshape(rows_here, panel_width)
    )
    column_panel = lax.all_gather(hidden, "tok", axis=0, tiled=True)
    ffn_place = lax.axis_index("ffn")
    begin_col = slab_offset[0] - ffn_place * panel_width
    padded = jnp.pad(hidden, ((0, 0), (SLAB, SLAB)))
    leading_column = jnp.clip(begin_col + SLAB, 0, panel_width + SLAB)
    slab_piece = lax.dynamic_slice_in_dim(padded, leading_column, SLAB, 1).astype(jnp.float32)
    summed = lax.psum(slab_piece.astype(jnp.bfloat16), "ffn")
    row_panel = lax.all_to_all(summed, "tok", split_axis=1, concat_axis=0, tiled=True)
    product = lax.dot_general(
        row_panel, column_panel, (((0,), (0,)), ((), ())), preferred_element_type=jnp.float32
    )
    return product * (2.0 / column_panel.shape[0])


def solution(mesh):
    ffn, tok = mesh.shape["ffn"], mesh.shape["tok"]

    def body(tokens, gate_blocks, up_blocks, block_rows, slab_offset):
        if tok == 4 and ffn % 2 == 0 and block_rows.shape[0] % 2 == 0:
            return shards_split(ffn, tokens, gate_blocks, up_blocks, block_rows, slab_offset)
        return shards(tokens, gate_blocks, up_blocks, block_rows, slab_offset)

    in_specs = (
        P(("grp", "tok"), "ffn"),
        P(("grp", "tok"), "ffn"),
        P(("grp", "tok"), "ffn"),
        P(("grp", "ffn"), None),
        P("grp"),
    )
    out_specs = P(("grp", "tok"), "ffn")
    return jax.shard_map(body, mesh=mesh, in_specs=in_specs, out_specs=out_specs, check_vma=False)
```

```python
import functools

import jax
import jax.numpy as jnp
from jax import lax
from jax.experimental import pallas as pl
from jax.experimental.pallas import tpu as pltpu
from jax.sharding import PartitionSpec as P

BLOCK = 128
SLAB = 4096
MESH = pl.DeviceIdType.MESH
ANY = pl.BlockSpec(memory_space=pl.ANY)


def remote(src, dst, send, recv, **where):
    return pltpu.make_async_remote_copy(
        src_ref=src, dst_ref=dst, send_sem=send, recv_sem=recv, device_id=where, device_id_type=MESH
    )


def greet(others, z_there):
    barrier = pltpu.get_barrier_semaphore()
    for where in others:
        pl.semaphore_signal(barrier, inc=1, device_id=where, device_id_type=MESH)
    for there, where in z_there:
        @pl.when(there)
        def _():
            pl.semaphore_signal(barrier, inc=1, device_id=where, device_id_type=MESH)
    count = len(others)
    for there, _ in z_there:
        count = count + jnp.where(there, 1, 0)
    pl.semaphore_wait(barrier, count)


def places():
    f, t = lax.axis_index("ffn"), lax.axis_index("tok")
    z, c = f // 2, f % 2
    y, x = t // 2, t % 2
    return f, t, z, c, y, x


def spread(chips, tok_ref, gate_ref, up_ref, t_ref, g_ref, u_ref,
           w_send, w_recv, l_sem, x_send, x_recv, c_send, c_recv, up_send, up_recv, dn_send, dn_recv):
    f, t, z, c, y, x = places()
    half = g_ref.shape[2]
    xn, yn, dn = y * 2 + 1 - x, (1 - y) * 2 + x, (1 - y) * 2 + 1 - x
    partner = z * 2 + 1 - c
    above, below = f + 2, f - 2
    greet(
        [dict(tok=xn), dict(tok=yn), dict(tok=dn), dict(ffn=partner)],
        [(z < chips - 1, dict(ffn=above)), (z > 0, dict(ffn=below))],
    )
    ends = []
    own = t_ref.at[f, x]
    cx = remote(tok_ref, own, x_send, x_recv, tok=xn)
    cx.start()

    def up(src, dst, zs, j):
        return remote(src, dst, up_send.at[zs, j], up_recv.at[zs, j], ffn=above)

    def down(src, dst, zs, j):
        return remote(src, dst, dn_send.at[zs, j], dn_recv.at[zs, j], ffn=below)

    def across(src, dst, zs, j):
        return remote(src, dst, c_send.at[zs, j], c_recv.at[zs, j], ffn=partner)

    def pass_on(src, dst, zs, j, go_up, go_down):
        if go_up is not None:
            @pl.when(go_up)
            def _():
                up(src, dst, zs, j).start()
        if go_down is not None:
            @pl.when(go_down)
            def _():
                down(src, dst, zs, j).start()
        across(src, dst, zs, j).start()

    pass_on(tok_ref, own, z, 0, z < chips - 1, z > 0)
    copies = []
    for k, (there, x_there) in enumerate(((xn, 1 - x), (yn, x), (dn, 1 - x))):
        cols = pl.ds(pl.multiple_of(x_there * half, BLOCK), half)
        for m, (src, dst) in enumerate(((gate_ref, g_ref), (up_ref, u_ref))):
            copy = remote(src.at[:, cols], dst.at[t], w_send.at[k, m], w_recv.at[k, m], tok=there)
            copy.start()
            copies.append(copy)
    cols = pl.ds(pl.multiple_of(x * half, BLOCK), half)
    locals_ = [
        pltpu.make_async_copy(tok_ref, own, l_sem.at[0]),
        pltpu.make_async_copy(gate_ref.at[:, cols], g_ref.at[t], l_sem.at[1]),
        pltpu.make_async_copy(up_ref.at[:, cols], u_ref.at[t], l_sem.at[2]),
    ]
    for copy in locals_:
        copy.start()
    other = t_ref.at[f, 1 - x]
    remote(tok_ref, other, x_send, x_recv, tok=xn).wait_recv()
    pass_on(other, other, z, 1, z < chips - 1, z > 0)
    for k in range(1, chips):
        for j in range(2):
            xs = x if j == 0 else 1 - x

            @pl.when(z >= k)
            def _():
                piece = t_ref.at[f - 2 * k, xs]
                up(piece, piece, z - k, j).wait_recv()
                pass_on(piece, piece, z - k, j, z < chips - 1, None)

            @pl.when(z + k < chips)
            def _():
                piece = t_ref.at[f + 2 * k, xs]
                down(piece, piece, z + k, j).wait_recv()
                pass_on(piece, piece, z + k, j, None, z > 0)

    for zs in range(chips):
        for j in range(2):
            xs = x if j == 0 else 1 - x
            got = t_ref.at[zs * 2 + 1 - c, xs]
            across(got, got, zs, j).wait_recv()
            across(got, got, zs, j).wait_send()

            @pl.when((zs <= z) & (z < chips - 1))
            def _():
                up(got, got, zs, j).wait_send()

            @pl.when((zs >= z) & (z > 0))
            def _():
                down(got, got, zs, j).wait_send()

    cx.wait_send()
    for copy in locals_:
        copy.wait()
    for copy in copies:
        copy.wait()


CHUNKS = 4


def join(chips, h_ref, s_ref, p_ref, r_ref, a, b, d, e, pin, qin, pout, qout,
         l_sem, send, recv, b_sem, d_send, d_recv, p_send, p_recv, q_send, q_recv, r_send, r_recv):
    f, t, z, c, y, x = places()
    rows, half = h_ref.shape
    xn, yn = y * 2 + 1 - x, (1 - y) * 2 + x
    partner = z * 2 + 1 - c
    above, below = f + 2, f - 2
    has_up, has_down = z < chips - 1, z > 0
    greet(
        [dict(tok=xn), dict(tok=yn), dict(ffn=partner)],
        [(has_up, dict(ffn=above)), (has_down, dict(ffn=below))],
    )
    cut = rows // 2

    def part(yy, xx, s):
        return p_ref.at[
            pl.ds(pl.multiple_of(yy * rows + s * cut, 16), cut),
            pl.ds(pl.multiple_of(xx * half, BLOCK), half),
        ]

    def copy(src, yy, xx, s, n, there):
        return remote(src, part(yy, xx, s), send.at[n], recv.at[n], tok=there)

    own = [h_ref.at[pl.ds(s * cut, cut)] for s in range(2)]
    sent = [
        copy(own[0], y, x, 0, 0, xn), copy(own[1], y, x, 1, 2, yn),
        copy(own[1], y, x, 1, 1, xn), copy(own[0], y, x, 0, 3, yn),
    ]
    mine, theirs = (pl.ds(pl.multiple_of(k * cut, 16), cut) for k in (c, 1 - c))
    swap = remote(s_ref.at[:, theirs], b, b_sem.at[0], b_sem.at[1], ffn=partner)
    swap.start()
    load = pltpu.make_async_copy(s_ref.at[:, mine], a, l_sem.at[1])
    load.start()
    sent[0].start()
    sent[1].start()
    sent[3].start()
    local = pltpu.make_async_copy(
        h_ref,
        p_ref.at[pl.ds(pl.multiple_of(y * rows, 16), rows), pl.ds(pl.multiple_of(x * half, BLOCK), half)],
        l_sem.at[0],
    )
    local.start()
    load.wait()
    swap.wait()

    strip = cut // CHUNKS

    def strip_of(k):
        return pl.ds(pl.multiple_of(k * strip, 16), strip)

    @pl.loop(0, CHUNKS)
    def _(k):
        a[:, strip_of(k)] = a[:, strip_of(k)] + b[:, strip_of(k)]

    over = [
        remote(a.at[yy * 2 + 1 - x], d.at[yy], d_send.at[yy], d_recv.at[yy], tok=xn) for yy in range(2)
    ]
    for o in over:
        o.start()
    for o in over:
        o.wait()
    sent[2].start()

    @pl.loop(0, CHUNKS)
    def _(k):
        for yy in range(2):
            e[yy, strip_of(k)] = a[yy * 2 + x, strip_of(k)] + d[yy, strip_of(k)]

    def rise(k):
        return remote(pout.at[:, strip_of(k)], pin.at[:, strip_of(k)], p_send.at[k], p_recv.at[k], ffn=above)

    def fall(k):
        return remote(qout.at[:, strip_of(k)], qin.at[:, strip_of(k)], q_send.at[k], q_recv.at[k], ffn=below)

    def line(first, last):
        for step in range(first, last):
            k = step - z

            @pl.when((k >= 0) & (k < CHUNKS))
            def _():
                @pl.when(z == 0)
                def _():
                    pout[:, strip_of(k)] = e[:, strip_of(k)]

                @pl.when(has_down)
                def _():
                    rise(k).wait_recv()
                    pout[:, strip_of(k)] = e[:, strip_of(k)] + pin[:, strip_of(k)]

                @pl.when(has_up)
                def _():
                    rise(k).start()

            n = step - (chips - 1 - z)

            @pl.when((n >= 0) & (n < CHUNKS))
            def _():
                @pl.when(z == chips - 1)
                def _():
                    qout[:, strip_of(n)] = e[:, strip_of(n)]

                @pl.when(has_up)
                def _():
                    fall(n).wait_recv()
                    qout[:, strip_of(n)] = e[:, strip_of(n)] + qin[:, strip_of(n)]

                @pl.when(has_down)
                def _():
                    fall(n).start()

    line(0, 2)
    via_x = part(y, 1 - x, 0)
    copy(via_x, y, 1 - x, 0, 0, xn).wait_recv()
    fy = copy(via_x, y, 1 - x, 0, 4, yn)
    fy.start()
    line(2, CHUNKS + chips - 1)

    @pl.loop(0, CHUNKS)
    def _(k):
        @pl.when(has_up)
        def _():
            e[:, strip_of(k)] = pout[:, strip_of(k)] + qin[:, strip_of(k)]

        @pl.when(z == chips - 1)
        def _():
            e[:, strip_of(k)] = pout[:, strip_of(k)]

    def slab_rows(yy):
        return r_ref.at[pl.ds(pl.multiple_of(yy * rows + c * cut, 16), cut)]

    to_y = remote(e.at[1 - y], slab_rows(y), r_send.at[0], r_recv.at[0], tok=yn)
    to_y.start()
    to_core = remote(e.at[y], slab_rows(y), r_send.at[1], r_recv.at[1], ffn=partner)
    to_core.start()
    keep = pltpu.make_async_copy(e.at[y], slab_rows(y), l_sem.at[2])
    keep.start()
    via_y = part(1 - y, x, 1)
    copy(via_y, 1 - y, x, 1, 2, yn).wait_recv()
    fx = copy(via_y, 1 - y, x, 1, 5, xn)
    fx.start()
    from_y = slab_rows(1 - y)
    remote(e.at[1 - y], from_y, r_send.at[0], r_recv.at[0], tok=yn).wait_recv()
    again = remote(from_y, from_y, r_send.at[2], r_recv.at[2], ffn=partner)
    again.start()
    to_y.wait_send()
    to_core.wait()
    keep.wait()
    again.wait()

    @pl.loop(0, CHUNKS)
    def _(k):
        @pl.when(has_up)
        def _():
            rise(k).wait_send()

        @pl.when(has_down)
        def _():
            fall(k).wait_send()

    sent[2].wait_recv()
    sent[3].wait_recv()
    fy.wait()
    fx.wait()
    for s in sent:
        s.wait_send()
    local.wait()


def hidden_kernel(per, rows_ref, begin_ref, t_ref, g_ref, u_ref, h_ref, s_ref):
    i = pl.program_id(0)
    depth = g_ref.shape[0]
    tiles = []
    for k in range(depth // BLOCK):
        r = rows_ref[i, k]
        tile = t_ref[r // per, :, :, pl.ds(pl.multiple_of((r % per) * BLOCK, BLOCK), BLOCK)]
        tiles.append(tile.reshape(-1, BLOCK))
    picked = jnp.concatenate(tiles, axis=1)
    weights = jnp.concatenate([g_ref[...], u_ref[...]], axis=1)
    both = jnp.dot(picked, weights, preferred_element_type=jnp.float32)
    gate, up = both[:, :BLOCK], both[:, BLOCK:]
    hidden = (gate / (1.0 + jnp.exp(-gate)) * up).astype(h_ref.dtype)
    h_ref[...] = hidden

    @pl.when(i == 0)
    def _():
        s_ref[...] = jnp.zeros_like(s_ref)

    wide = s_ref.shape[2] // BLOCK
    at = i - begin_ref[0]

    @pl.when((at >= 0) & (at < wide * s_ref.shape[0]))
    def _():
        s_ref[at // wide, :, pl.ds(pl.multiple_of((at % wide) * BLOCK, BLOCK), BLOCK)] = hidden


def product_kernel(scale, a_ref, b_ref, o_ref):
    o_ref[...] = jnp.dot(a_ref[...], b_ref[...], preferred_element_type=jnp.float32) * scale


def params(**more):
    return pltpu.CompilerParams(**more)


def shards_split(ffn, tokens, gate_blocks, up_blocks, block_rows, slab_offset):
    rows, feats = tokens.shape
    depth, panel = gate_blocks.shape
    half = panel // 2
    chips = ffn // 2
    bf = jnp.bfloat16
    dma = pltpu.SemaphoreType.DMA
    shape = jax.ShapeDtypeStruct
    spread_tokens, gates, ups = pl.pallas_call(
        functools.partial(spread, chips),
        out_shape=(shape((ffn, 2, rows, feats), bf), shape((4, depth, half), bf), shape((4, depth, half), bf)),
        in_specs=[ANY] * 3,
        out_specs=(ANY,) * 3,
        scratch_shapes=[
            dma((3, 2)), dma((3, 2)), dma((3,)), dma, dma,
            dma((chips, 2)), dma((chips, 2)), dma((chips, 2)),
            dma((chips, 2)), dma((chips, 2)), dma((chips, 2)),
        ],
        compiler_params=params(collective_id=0, has_side_effects=True),
        name="spread",
    )(tokens, gate_blocks, up_blocks)
    t = lax.axis_index("tok")
    f = lax.axis_index("ffn")
    count = half // BLOCK
    rows_here = lax.dynamic_slice_in_dim(block_rows, (t % 2) * count, count, 0)
    wide = SLAB // 4
    begin = slab_offset // BLOCK - (f * 2 + t % 2) * count
    hidden, slab = pl.pallas_call(
        functools.partial(hidden_kernel, feats // BLOCK),
        out_shape=(shape((2 * rows, half), bf), shape((4, 2 * rows, wide), bf)),
        grid_spec=pltpu.PrefetchScalarGridSpec(
            num_scalar_prefetch=2,
            grid=(count,),
            in_specs=[
                pl.BlockSpec(memory_space=pltpu.VMEM),
                pl.BlockSpec((4 * depth, BLOCK), lambda i, r, b: (0, i)),
                pl.BlockSpec((4 * depth, BLOCK), lambda i, r, b: (0, i)),
            ],
            out_specs=(
                pl.BlockSpec((2 * rows, BLOCK), lambda i, r, b: (0, i)),
                pl.BlockSpec((4, 2 * rows, wide), lambda i, r, b: (0, 0, 0)),
            ),
        ),
        compiler_params=params(vmem_limit_bytes=48 * 1024 * 1024),
        name="hidden",
    )(rows_here, begin, spread_tokens, gates.reshape(4 * depth, half), ups.reshape(4 * depth, half))
    vmem = pltpu.VMEM
    whole, row_panel = pl.pallas_call(
        functools.partial(join, chips),
        out_shape=(shape((4 * rows, panel), bf), shape((4 * rows, wide), bf)),
        in_specs=[ANY] * 2,
        out_specs=(ANY,) * 2,
        scratch_shapes=[
            vmem((4, rows, wide), bf), vmem((4, rows, wide), bf),
            *[vmem((2, rows, wide), bf) for _ in range(6)],
            dma((3,)), dma((6,)), dma((6,)), dma((2,)), dma((2,)), dma((2,)),
            *[dma((CHUNKS,)) for _ in range(4)],
            dma((3,)), dma((3,)),
        ],
        compiler_params=params(
            collective_id=1, has_side_effects=True, vmem_limit_bytes=32 * 1024 * 1024
        ),
        name="join",
    )(hidden, slab)
    row_panel = row_panel.T
    tile = 512 if panel % 512 == 0 else BLOCK
    return pl.pallas_call(
        functools.partial(product_kernel, 2.0 / (4 * rows)),
        out_shape=shape((wide, panel), jnp.float32),
        grid=(panel // tile,),
        in_specs=[
            pl.BlockSpec((wide, 4 * rows), lambda i: (0, 0)),
            pl.BlockSpec((4 * rows, tile), lambda i: (0, i)),
        ],
        out_specs=pl.BlockSpec((wide, tile), lambda i: (0, i)),
        compiler_params=params(vmem_limit_bytes=48 * 1024 * 1024),
        name="product",
    )(row_panel, whole)


def shards(tokens, gate_blocks, up_blocks, block_rows, slab_offset):
    rows_here = tokens.shape[0]
    column_count = block_rows.shape[0]
    whole = lax.all_gather(tokens, "ffn", axis=1, tiled=True)
    feature_tiles = whole.reshape(rows_here, -1, BLOCK)
    chosen_entries = jnp.take(feature_tiles, block_rows, axis=1)
    pieces = (
        lax.all_gather(gate_blocks, "tok", axis=0, tiled=True),
        lax.all_gather(up_blocks, "tok", axis=0, tiled=True),
    )
    block_count = pieces[0].shape[0] // BLOCK
    gate_segment = pieces[0].reshape(block_count, BLOCK, column_count, BLOCK)
    up_segment = pieces[1].reshape(block_count, BLOCK, column_count, BLOCK)
    gate_add = jnp.einsum(
        "aqdh,dhqz->aqz", chosen_entries, gate_segment, preferred_element_type=jnp.float32
    )
    up_increment = jnp.einsum(
        "aqdh,dhqz->aqz", chosen_entries, up_segment, preferred_element_type=jnp.float32
    )
    panel_width = column_count * BLOCK
    hidden = (
        (jax.nn.silu(gate_add) * up_increment).astype(jnp.bfloat16).reshape(rows_here, panel_width)
    )
    column_panel = lax.all_gather(hidden, "tok", axis=0, tiled=True)
    ffn_place = lax.axis_index("ffn")
    begin_col = slab_offset[0] - ffn_place * panel_width
    padded = jnp.pad(hidden, ((0, 0), (SLAB, SLAB)))
    leading_column = jnp.clip(begin_col + SLAB, 0, panel_width + SLAB)
    slab_piece = lax.dynamic_slice_in_dim(padded, leading_column, SLAB, 1).astype(jnp.float32)
    summed = lax.psum(slab_piece.astype(jnp.bfloat16), "ffn")
    row_panel = lax.all_to_all(summed, "tok", split_axis=1, concat_axis=0, tiled=True)
    product = lax.dot_general(
        row_panel, column_panel, (((0,), (0,)), ((), ())), preferred_element_type=jnp.float32
    )
    return product * (2.0 / column_panel.shape[0])


def solution(mesh):
    ffn, tok = mesh.shape["ffn"], mesh.shape["tok"]

    def body(tokens, gate_blocks, up_blocks, block_rows, slab_offset):
        if tok == 4 and ffn % 2 == 0 and block_rows.shape[0] % 2 == 0:
            return shards_split(ffn, tokens, gate_blocks, up_blocks, block_rows, slab_offset)
        return shards(tokens, gate_blocks, up_blocks, block_rows, slab_offset)

    in_specs = (
        P(("grp", "tok"), "ffn"),
        P(("grp", "tok"), "ffn"),
        P(("grp", "tok"), "ffn"),
        P(("grp", "ffn"), None),
        P("grp"),
    )
    out_specs = P(("grp", "tok"), "ffn")
    return jax.shard_map(body, mesh=mesh, in_specs=in_specs, out_specs=out_specs, check_vma=False)
```

```python
import functools

import jax
import jax.numpy as jnp
from jax import lax
from jax.experimental import pallas as pl
from jax.experimental.pallas import tpu as pltpu
from jax.sharding import PartitionSpec as P

BLOCK = 128
SLAB = 4096
MESH = pl.DeviceIdType.MESH
ANY = pl.BlockSpec(memory_space=pl.ANY)


def remote(src, dst, send, recv, **where):
    return pltpu.make_async_remote_copy(
        src_ref=src, dst_ref=dst, send_sem=send, recv_sem=recv, device_id=where, device_id_type=MESH
    )


def greet(others, z_there):
    barrier = pltpu.get_barrier_semaphore()
    for where in others:
        pl.semaphore_signal(barrier, inc=1, device_id=where, device_id_type=MESH)
    for there, where in z_there:
        @pl.when(there)
        def _():
            pl.semaphore_signal(barrier, inc=1, device_id=where, device_id_type=MESH)
    count = len(others)
    for there, _ in z_there:
        count = count + jnp.where(there, 1, 0)
    pl.semaphore_wait(barrier, count)


def places():
    f, t = lax.axis_index("ffn"), lax.axis_index("tok")
    z, c = f // 2, f % 2
    y, x = t // 2, t % 2
    return f, t, z, c, y, x


def spread(chips, tok_ref, gate_ref, up_ref, t_ref, g_ref, u_ref,
           w_send, w_recv, l_sem, x_send, x_recv, c_send, c_recv, up_send, up_recv, dn_send, dn_recv):
    f, t, z, c, y, x = places()
    half = g_ref.shape[2]
    xn, yn = y * 2 + 1 - x, (1 - y) * 2 + x
    partner = z * 2 + 1 - c
    above, below = f + 2, f - 2
    greet(
        [dict(tok=xn), dict(tok=yn), dict(ffn=partner)],
        [(z < chips - 1, dict(ffn=above)), (z > 0, dict(ffn=below))],
    )
    ends = []
    own = t_ref.at[f, x]
    cx = remote(tok_ref, own, x_send, x_recv, tok=xn)
    cx.start()

    def up(src, dst, zs, j):
        return remote(src, dst, up_send.at[zs, j], up_recv.at[zs, j], ffn=above)

    def down(src, dst, zs, j):
        return remote(src, dst, dn_send.at[zs, j], dn_recv.at[zs, j], ffn=below)

    def across(src, dst, zs, j):
        return remote(src, dst, c_send.at[zs, j], c_recv.at[zs, j], ffn=partner)

    def pass_on(src, dst, zs, j, go_up, go_down):
        if go_up is not None:
            @pl.when(go_up)
            def _():
                up(src, dst, zs, j).start()
        if go_down is not None:
            @pl.when(go_down)
            def _():
                down(src, dst, zs, j).start()
        across(src, dst, zs, j).start()

    pass_on(tok_ref, own, z, 0, z < chips - 1, z > 0)
    here = pl.ds(pl.multiple_of(x * half, BLOCK), half)
    there = pl.ds(pl.multiple_of((1 - x) * half, BLOCK), half)
    pairs = ((gate_ref, g_ref), (up_ref, u_ref))
    over_y = [remote(s.at[:, here], d.at[t], w_send.at[0, m], w_recv.at[0, m], tok=yn) for m, (s, d) in enumerate(pairs)]
    over_x = [remote(s.at[:, there], d.at[t], w_send.at[1, m], w_recv.at[1, m], tok=xn) for m, (s, d) in enumerate(pairs)]
    onward = [remote(d.at[xn], d.at[xn], w_send.at[2, m], w_recv.at[2, m], tok=yn) for m, (s, d) in enumerate(pairs)]
    for copy in over_y:
        copy.start()
    locals_ = [
        pltpu.make_async_copy(tok_ref, own, l_sem.at[0]),
        pltpu.make_async_copy(gate_ref.at[:, here], g_ref.at[t], l_sem.at[1]),
        pltpu.make_async_copy(up_ref.at[:, here], u_ref.at[t], l_sem.at[2]),
    ]
    for copy in locals_:
        copy.start()
    other = t_ref.at[f, 1 - x]
    remote(tok_ref, other, x_send, x_recv, tok=xn).wait_recv()
    pass_on(other, other, z, 1, z < chips - 1, z > 0)
    over_x[0].start()
    for k in range(1, chips):
        for j in range(2):
            xs = x if j == 0 else 1 - x

            @pl.when(z >= k)
            def _():
                piece = t_ref.at[f - 2 * k, xs]
                up(piece, piece, z - k, j).wait_recv()
                pass_on(piece, piece, z - k, j, z < chips - 1, None)

            @pl.when(z + k < chips)
            def _():
                piece = t_ref.at[f + 2 * k, xs]
                down(piece, piece, z + k, j).wait_recv()
                pass_on(piece, piece, z + k, j, None, z > 0)

        if k < 3:
            over_x[k - 1].wait_recv()
            onward[k - 1].start()
            if k == 1:
                over_x[0].wait_send()
                over_x[1].start()

    for zs in range(chips):
        for j in range(2):
            xs = x if j == 0 else 1 - x
            got = t_ref.at[zs * 2 + 1 - c, xs]
            across(got, got, zs, j).wait_recv()
            across(got, got, zs, j).wait_send()

            @pl.when((zs <= z) & (z < chips - 1))
            def _():
                up(got, got, zs, j).wait_send()

            @pl.when((zs >= z) & (z > 0))
            def _():
                down(got, got, zs, j).wait_send()

    cx.wait_send()
    for copy in locals_:
        copy.wait()
    for copy in over_y + onward:
        copy.wait()
    over_x[1].wait_send()


CHUNKS = 4


def join(chips, h_ref, s_ref, p_ref, r_ref, a, b, d, e, pin, qin, pout, qout,
         l_sem, send, recv, b_sem, d_send, d_recv, p_send, p_recv, q_send, q_recv, r_send, r_recv):
    f, t, z, c, y, x = places()
    rows, half = h_ref.shape
    xn, yn = y * 2 + 1 - x, (1 - y) * 2 + x
    partner = z * 2 + 1 - c
    above, below = f + 2, f - 2
    has_up, has_down = z < chips - 1, z > 0
    greet(
        [dict(tok=xn), dict(tok=yn), dict(ffn=partner)],
        [(has_up, dict(ffn=above)), (has_down, dict(ffn=below))],
    )
    cut = rows // 2

    first = rows * 9 // 16
    spans = ((0, first), (first, rows - first))

    def part(yy, xx, s):
        return p_ref.at[
            pl.ds(pl.multiple_of(yy * rows + spans[s][0], 16), spans[s][1]),
            pl.ds(pl.multiple_of(xx * half, BLOCK), half),
        ]

    def copy(src, yy, xx, s, n, there):
        return remote(src, part(yy, xx, s), send.at[n], recv.at[n], tok=there)

    own = [h_ref.at[pl.ds(*span)] for span in spans]
    sent = [
        copy(own[0], y, x, 0, 0, xn), copy(own[1], y, x, 1, 2, yn),
        copy(own[1], y, x, 1, 1, xn), copy(own[0], y, x, 0, 3, yn),
    ]
    mine, theirs = (pl.ds(pl.multiple_of(k * cut, 16), cut) for k in (c, 1 - c))
    swap = remote(s_ref.at[:, theirs], b, b_sem.at[0], b_sem.at[1], ffn=partner)
    swap.start()
    load = pltpu.make_async_copy(s_ref.at[:, mine], a, l_sem.at[1])
    load.start()
    sent[0].start()
    sent[1].start()
    sent[3].start()
    local = pltpu.make_async_copy(
        h_ref,
        p_ref.at[pl.ds(pl.multiple_of(y * rows, 16), rows), pl.ds(pl.multiple_of(x * half, BLOCK), half)],
        l_sem.at[0],
    )
    local.start()
    load.wait()
    swap.wait()

    strip = cut // CHUNKS

    def strip_of(k):
        return pl.ds(pl.multiple_of(k * strip, 16), strip)

    @pl.loop(0, CHUNKS)
    def _(k):
        a[:, strip_of(k)] = a[:, strip_of(k)] + b[:, strip_of(k)]

    over = [
        remote(a.at[yy * 2 + 1 - x], d.at[yy], d_send.at[yy], d_recv.at[yy], tok=xn) for yy in range(2)
    ]
    for o in over:
        o.start()
    for o in over:
        o.wait()
    sent[2].start()

    @pl.loop(0, CHUNKS)
    def _(k):
        for yy in range(2):
            e[yy, strip_of(k)] = a[yy * 2 + x, strip_of(k)] + d[yy, strip_of(k)]

    def rise(k):
        return remote(pout.at[:, strip_of(k)], pin.at[:, strip_of(k)], p_send.at[k], p_recv.at[k], ffn=above)

    def fall(k):
        return remote(qout.at[:, strip_of(k)], qin.at[:, strip_of(k)], q_send.at[k], q_recv.at[k], ffn=below)

    def line(first, last):
        for step in range(first, last):
            k = step - z

            @pl.when((k >= 0) & (k < CHUNKS))
            def _():
                @pl.when(z == 0)
                def _():
                    pout[:, strip_of(k)] = e[:, strip_of(k)]

                @pl.when(has_down)
                def _():
                    rise(k).wait_recv()
                    pout[:, strip_of(k)] = e[:, strip_of(k)] + pin[:, strip_of(k)]

                @pl.when(has_up)
                def _():
                    rise(k).start()

            n = step - (chips - 1 - z)

            @pl.when((n >= 0) & (n < CHUNKS))
            def _():
                @pl.when(z == chips - 1)
                def _():
                    qout[:, strip_of(n)] = e[:, strip_of(n)]

                @pl.when(has_up)
                def _():
                    fall(n).wait_recv()
                    qout[:, strip_of(n)] = e[:, strip_of(n)] + qin[:, strip_of(n)]

                @pl.when(has_down)
                def _():
                    fall(n).start()

    line(0, 2)
    via_x = part(y, 1 - x, 0)
    copy(via_x, y, 1 - x, 0, 0, xn).wait_recv()
    fy = copy(via_x, y, 1 - x, 0, 4, yn)
    fy.start()
    line(2, CHUNKS + chips - 1)

    @pl.loop(0, CHUNKS)
    def _(k):
        @pl.when(has_up)
        def _():
            e[:, strip_of(k)] = pout[:, strip_of(k)] + qin[:, strip_of(k)]

        @pl.when(z == chips - 1)
        def _():
            e[:, strip_of(k)] = pout[:, strip_of(k)]

    def slab_rows(yy):
        return r_ref.at[pl.ds(pl.multiple_of(yy * rows + c * cut, 16), cut)]

    to_y = remote(e.at[1 - y], slab_rows(y), r_send.at[0], r_recv.at[0], tok=yn)
    to_y.start()
    to_core = remote(e.at[y], slab_rows(y), r_send.at[1], r_recv.at[1], ffn=partner)
    to_core.start()
    keep = pltpu.make_async_copy(e.at[y], slab_rows(y), l_sem.at[2])
    keep.start()
    via_y = part(1 - y, x, 1)
    copy(via_y, 1 - y, x, 1, 2, yn).wait_recv()
    fx = copy(via_y, 1 - y, x, 1, 5, xn)
    fx.start()
    from_y = slab_rows(1 - y)
    remote(e.at[1 - y], from_y, r_send.at[0], r_recv.at[0], tok=yn).wait_recv()
    again = remote(from_y, from_y, r_send.at[2], r_recv.at[2], ffn=partner)
    again.start()
    to_y.wait_send()
    to_core.wait()
    keep.wait()
    again.wait()

    @pl.loop(0, CHUNKS)
    def _(k):
        @pl.when(has_up)
        def _():
            rise(k).wait_send()

        @pl.when(has_down)
        def _():
            fall(k).wait_send()

    sent[2].wait_recv()
    sent[3].wait_recv()
    fy.wait()
    fx.wait()
    for s in sent:
        s.wait_send()
    local.wait()


def hidden_kernel(per, rows_ref, begin_ref, t_ref, g_ref, u_ref, h_ref, s_ref):
    i = pl.program_id(0)
    depth, width = g_ref.shape
    many = width // BLOCK
    wide = s_ref.shape[2] // BLOCK

    @pl.when(i == 0)
    def _():
        s_ref[...] = jnp.zeros_like(s_ref)

    for n in range(many):
        column = i * many + n
        span = pl.ds(n * BLOCK, BLOCK)
        tiles = []
        for k in range(depth // BLOCK):
            r = rows_ref[column, k]
            tile = t_ref[r // per, :, :, pl.ds(pl.multiple_of((r % per) * BLOCK, BLOCK), BLOCK)]
            tiles.append(tile.reshape(-1, BLOCK))
        picked = jnp.concatenate(tiles, axis=1)
        weights = jnp.concatenate([g_ref[:, span], u_ref[:, span]], axis=1)
        both = jnp.dot(picked, weights, preferred_element_type=jnp.float32)
        gate, up = both[:, :BLOCK], both[:, BLOCK:]
        hidden = (gate / (1.0 + jnp.exp(-gate)) * up).astype(h_ref.dtype)
        h_ref[:, span] = hidden
        at = column - begin_ref[0]

        @pl.when((at >= 0) & (at < wide * s_ref.shape[0]))
        def _():
            s_ref[at // wide, :, pl.ds(pl.multiple_of((at % wide) * BLOCK, BLOCK), BLOCK)] = hidden


def product_kernel(scale, a_ref, b_ref, o_ref, turned):
    @pl.when(pl.program_id(0) == 0)
    def _():
        turned[...] = a_ref[...].T

    o_ref[...] = jnp.dot(turned[...], b_ref[...], preferred_element_type=jnp.float32) * scale


def params(**more):
    return pltpu.CompilerParams(**more)


def shards_split(ffn, tokens, gate_blocks, up_blocks, block_rows, slab_offset):
    rows, feats = tokens.shape
    depth, panel = gate_blocks.shape
    half = panel // 2
    chips = ffn // 2
    bf = jnp.bfloat16
    dma = pltpu.SemaphoreType.DMA
    shape = jax.ShapeDtypeStruct
    spread_tokens, gates, ups = pl.pallas_call(
        functools.partial(spread, chips),
        out_shape=(shape((ffn, 2, rows, feats), bf), shape((4, depth, half), bf), shape((4, depth, half), bf)),
        in_specs=[ANY] * 3,
        out_specs=(ANY,) * 3,
        scratch_shapes=[
            dma((3, 2)), dma((3, 2)), dma((3,)), dma, dma,
            dma((chips, 2)), dma((chips, 2)), dma((chips, 2)),
            dma((chips, 2)), dma((chips, 2)), dma((chips, 2)),
        ],
        compiler_params=params(collective_id=0, has_side_effects=True),
        name="spread",
    )(tokens, gate_blocks, up_blocks)
    t = lax.axis_index("tok")
    f = lax.axis_index("ffn")
    count = half // BLOCK
    rows_here = lax.dynamic_slice_in_dim(block_rows, (t % 2) * count, count, 0)
    many = 2 if count % 2 == 0 else 1
    wide = SLAB // 4
    begin = slab_offset // BLOCK - (f * 2 + t % 2) * count
    hidden, slab = pl.pallas_call(
        functools.partial(hidden_kernel, feats // BLOCK),
        out_shape=(shape((2 * rows, half), bf), shape((4, 2 * rows, wide), bf)),
        grid_spec=pltpu.PrefetchScalarGridSpec(
            num_scalar_prefetch=2,
            grid=(count // many,),
            in_specs=[
                pl.BlockSpec(memory_space=pltpu.VMEM),
                pl.BlockSpec((4 * depth, many * BLOCK), lambda i, r, b: (0, i)),
                pl.BlockSpec((4 * depth, many * BLOCK), lambda i, r, b: (0, i)),
            ],
            out_specs=(
                pl.BlockSpec((2 * rows, many * BLOCK), lambda i, r, b: (0, i)),
                pl.BlockSpec((4, 2 * rows, wide), lambda i, r, b: (0, 0, 0)),
            ),
        ),
        compiler_params=params(vmem_limit_bytes=48 * 1024 * 1024),
        name="hidden",
    )(rows_here, begin, spread_tokens, gates.reshape(4 * depth, half), ups.reshape(4 * depth, half))
    vmem = pltpu.VMEM
    whole, row_panel = pl.pallas_call(
        functools.partial(join, chips),
        out_shape=(shape((4 * rows, panel), bf), shape((4 * rows, wide), bf)),
        in_specs=[ANY] * 2,
        out_specs=(ANY,) * 2,
        scratch_shapes=[
            vmem((4, rows, wide), bf), vmem((4, rows, wide), bf),
            *[vmem((2, rows, wide), bf) for _ in range(6)],
            dma((3,)), dma((6,)), dma((6,)), dma((2,)), dma((2,)), dma((2,)),
            *[dma((CHUNKS,)) for _ in range(4)],
            dma((3,)), dma((3,)),
        ],
        compiler_params=params(
            collective_id=1, has_side_effects=True, vmem_limit_bytes=32 * 1024 * 1024
        ),
        name="join",
    )(hidden, slab)
    tile = 512 if panel % 512 == 0 else BLOCK
    return pl.pallas_call(
        functools.partial(product_kernel, 2.0 / (4 * rows)),
        out_shape=shape((wide, panel), jnp.float32),
        grid=(panel // tile,),
        in_specs=[
            pl.BlockSpec((4 * rows, wide), lambda i: (0, 0)),
            pl.BlockSpec((4 * rows, tile), lambda i: (0, i)),
        ],
        out_specs=pl.BlockSpec((wide, tile), lambda i: (0, i)),
        scratch_shapes=[vmem((wide, 4 * rows), bf)],
        compiler_params=params(vmem_limit_bytes=48 * 1024 * 1024),
        name="product",
    )(row_panel, whole)


def shards(tokens, gate_blocks, up_blocks, block_rows, slab_offset):
    rows_here = tokens.shape[0]
    column_count = block_rows.shape[0]
    whole = lax.all_gather(tokens, "ffn", axis=1, tiled=True)
    feature_tiles = whole.reshape(rows_here, -1, BLOCK)
    chosen_entries = jnp.take(feature_tiles, block_rows, axis=1)
    pieces = (
        lax.all_gather(gate_blocks, "tok", axis=0, tiled=True),
        lax.all_gather(up_blocks, "tok", axis=0, tiled=True),
    )
    block_count = pieces[0].shape[0] // BLOCK
    gate_segment = pieces[0].reshape(block_count, BLOCK, column_count, BLOCK)
    up_segment = pieces[1].reshape(block_count, BLOCK, column_count, BLOCK)
    gate_add = jnp.einsum(
        "aqdh,dhqz->aqz", chosen_entries, gate_segment, preferred_element_type=jnp.float32
    )
    up_increment = jnp.einsum(
        "aqdh,dhqz->aqz", chosen_entries, up_segment, preferred_element_type=jnp.float32
    )
    panel_width = column_count * BLOCK
    hidden = (
        (jax.nn.silu(gate_add) * up_increment).astype(jnp.bfloat16).reshape(rows_here, panel_width)
    )
    column_panel = lax.all_gather(hidden, "tok", axis=0, tiled=True)
    ffn_place = lax.axis_index("ffn")
    begin_col = slab_offset[0] - ffn_place * panel_width
    padded = jnp.pad(hidden, ((0, 0), (SLAB, SLAB)))
    leading_column = jnp.clip(begin_col + SLAB, 0, panel_width + SLAB)
    slab_piece = lax.dynamic_slice_in_dim(padded, leading_column, SLAB, 1).astype(jnp.float32)
    summed = lax.psum(slab_piece.astype(jnp.bfloat16), "ffn")
    row_panel = lax.all_to_all(summed, "tok", split_axis=1, concat_axis=0, tiled=True)
    product = lax.dot_general(
        row_panel, column_panel, (((0,), (0,)), ((), ())), preferred_element_type=jnp.float32
    )
    return product * (2.0 / column_panel.shape[0])


def solution(mesh):
    ffn, tok = mesh.shape["ffn"], mesh.shape["tok"]

    def body(tokens, gate_blocks, up_blocks, block_rows, slab_offset):
        if tok == 4 and ffn >= 6 and ffn % 2 == 0 and block_rows.shape[0] % 2 == 0:
            return shards_split(ffn, tokens, gate_blocks, up_blocks, block_rows, slab_offset)
        return shards(tokens, gate_blocks, up_blocks, block_rows, slab_offset)

    in_specs = (
        P(("grp", "tok"), "ffn"),
        P(("grp", "tok"), "ffn"),
        P(("grp", "tok"), "ffn"),
        P(("grp", "ffn"), None),
        P("grp"),
    )
    out_specs = P(("grp", "tok"), "ffn")
    return jax.shard_map(body, mesh=mesh, in_specs=in_specs, out_specs=out_specs, check_vma=False)
```

```python
import functools

import jax
import jax.numpy as jnp
from jax import lax
from jax.experimental import pallas as pl
from jax.experimental.pallas import tpu as pltpu
from jax.sharding import PartitionSpec as P

BLOCK = 128
SLAB = 4096
MESH = pl.DeviceIdType.MESH
ANY = pl.BlockSpec(memory_space=pl.ANY)


def remote(src, dst, send, recv, **where):
    return pltpu.make_async_remote_copy(
        src_ref=src, dst_ref=dst, send_sem=send, recv_sem=recv, device_id=where, device_id_type=MESH
    )


def greet(others, z_there):
    barrier = pltpu.get_barrier_semaphore()
    for where in others:
        pl.semaphore_signal(barrier, inc=1, device_id=where, device_id_type=MESH)
    for there, where in z_there:
        @pl.when(there)
        def _():
            pl.semaphore_signal(barrier, inc=1, device_id=where, device_id_type=MESH)
    count = len(others)
    for there, _ in z_there:
        count = count + jnp.where(there, 1, 0)
    pl.semaphore_wait(barrier, count)


def places():
    f, t = lax.axis_index("ffn"), lax.axis_index("tok")
    z, c = f // 2, f % 2
    y, x = t // 2, t % 2
    return f, t, z, c, y, x


def spread(chips, tok_ref, gate_ref, up_ref, t_ref, g_ref, u_ref,
           w_send, w_recv, l_sem, x_send, x_recv, c_send, c_recv, up_send, up_recv, dn_send, dn_recv):
    f, t, z, c, y, x = places()
    half = g_ref.shape[2]
    xn, yn = y * 2 + 1 - x, (1 - y) * 2 + x
    partner = z * 2 + 1 - c
    above, below = f + 2, f - 2
    greet(
        [dict(tok=xn), dict(tok=yn), dict(ffn=partner)],
        [(z < chips - 1, dict(ffn=above)), (z > 0, dict(ffn=below))],
    )
    ends = []
    own = t_ref.at[f, x]
    cx = remote(tok_ref, own, x_send, x_recv, tok=xn)
    cx.start()

    def up(src, dst, zs, j):
        return remote(src, dst, up_send.at[zs, j], up_recv.at[zs, j], ffn=above)

    def down(src, dst, zs, j):
        return remote(src, dst, dn_send.at[zs, j], dn_recv.at[zs, j], ffn=below)

    def across(src, dst, zs, j):
        return remote(src, dst, c_send.at[zs, j], c_recv.at[zs, j], ffn=partner)

    def pass_on(src, dst, zs, j, go_up, go_down):
        if go_up is not None:
            @pl.when(go_up)
            def _():
                up(src, dst, zs, j).start()
        if go_down is not None:
            @pl.when(go_down)
            def _():
                down(src, dst, zs, j).start()
        across(src, dst, zs, j).start()

    pass_on(tok_ref, own, z, 0, z < chips - 1, z > 0)
    here = pl.ds(pl.multiple_of(x * half, BLOCK), half)
    there = pl.ds(pl.multiple_of((1 - x) * half, BLOCK), half)
    pairs = ((gate_ref, g_ref), (up_ref, u_ref))
    over_y = [remote(s.at[:, here], d.at[t], w_send.at[0, m], w_recv.at[0, m], tok=yn) for m, (s, d) in enumerate(pairs)]
    over_x = [remote(s.at[:, there], d.at[t], w_send.at[1, m], w_recv.at[1, m], tok=xn) for m, (s, d) in enumerate(pairs)]
    onward = [remote(d.at[xn], d.at[xn], w_send.at[2, m], w_recv.at[2, m], tok=yn) for m, (s, d) in enumerate(pairs)]
    for copy in over_y:
        copy.start()
    locals_ = [
        pltpu.make_async_copy(tok_ref, own, l_sem.at[0]),
        pltpu.make_async_copy(gate_ref.at[:, here], g_ref.at[t], l_sem.at[1]),
        pltpu.make_async_copy(up_ref.at[:, here], u_ref.at[t], l_sem.at[2]),
    ]
    for copy in locals_:
        copy.start()
    other = t_ref.at[f, 1 - x]
    remote(tok_ref, other, x_send, x_recv, tok=xn).wait_recv()
    pass_on(other, other, z, 1, z < chips - 1, z > 0)
    over_x[0].start()
    for k in range(1, chips):
        for j in range(2):
            xs = x if j == 0 else 1 - x

            @pl.when(z >= k)
            def _():
                piece = t_ref.at[f - 2 * k, xs]
                up(piece, piece, z - k, j).wait_recv()
                pass_on(piece, piece, z - k, j, z < chips - 1, None)

            @pl.when(z + k < chips)
            def _():
                piece = t_ref.at[f + 2 * k, xs]
                down(piece, piece, z + k, j).wait_recv()
                pass_on(piece, piece, z + k, j, None, z > 0)

        if k < 3:
            over_x[k - 1].wait_recv()
            onward[k - 1].start()
            if k == 1:
                over_x[0].wait_send()
                over_x[1].start()

    for zs in range(chips):
        for j in range(2):
            xs = x if j == 0 else 1 - x
            got = t_ref.at[zs * 2 + 1 - c, xs]
            across(got, got, zs, j).wait_recv()
            across(got, got, zs, j).wait_send()

            @pl.when((zs <= z) & (z < chips - 1))
            def _():
                up(got, got, zs, j).wait_send()

            @pl.when((zs >= z) & (z > 0))
            def _():
                down(got, got, zs, j).wait_send()

    cx.wait_send()
    for copy in locals_:
        copy.wait()
    for copy in over_y + onward:
        copy.wait()
    over_x[1].wait_send()


CHUNKS = 4


def join(chips, h_ref, s_ref, p_ref, r_ref, a, b, d, e, pin, qin, pout, qout,
         l_sem, send, recv, b_sem, d_send, d_recv, p_send, p_recv, q_send, q_recv, r_send, r_recv):
    f, t, z, c, y, x = places()
    rows, half = h_ref.shape
    xn, yn = y * 2 + 1 - x, (1 - y) * 2 + x
    partner = z * 2 + 1 - c
    above, below = f + 2, f - 2
    has_up, has_down = z < chips - 1, z > 0
    greet(
        [dict(tok=xn), dict(tok=yn), dict(ffn=partner)],
        [(has_up, dict(ffn=above)), (has_down, dict(ffn=below))],
    )
    cut = rows // 2

    first = rows * 9 // 16
    spans = ((0, first), (first, rows - first))

    def part(yy, xx, s):
        return p_ref.at[
            pl.ds(pl.multiple_of(yy * rows + spans[s][0], 16), spans[s][1]),
            pl.ds(pl.multiple_of(xx * half, BLOCK), half),
        ]

    def copy(src, yy, xx, s, n, there):
        return remote(src, part(yy, xx, s), send.at[n], recv.at[n], tok=there)

    own = [h_ref.at[pl.ds(*span)] for span in spans]
    sent = [
        copy(own[0], y, x, 0, 0, xn), copy(own[1], y, x, 1, 2, yn),
        copy(own[1], y, x, 1, 1, xn), copy(own[0], y, x, 0, 3, yn),
    ]
    mine, theirs = (pl.ds(pl.multiple_of(k * cut, 16), cut) for k in (c, 1 - c))
    swap = remote(s_ref.at[:, theirs], b, b_sem.at[0], b_sem.at[1], ffn=partner)
    swap.start()
    load = pltpu.make_async_copy(s_ref.at[:, mine], a, l_sem.at[1])
    load.start()
    sent[0].start()
    sent[1].start()
    sent[3].start()
    local = pltpu.make_async_copy(
        h_ref,
        p_ref.at[pl.ds(pl.multiple_of(y * rows, 16), rows), pl.ds(pl.multiple_of(x * half, BLOCK), half)],
        l_sem.at[0],
    )
    local.start()
    load.wait()
    swap.wait()

    strip = cut // CHUNKS

    def strip_of(k):
        return pl.ds(pl.multiple_of(k * strip, 16), strip)

    @pl.loop(0, CHUNKS)
    def _(k):
        a[:, strip_of(k)] = a[:, strip_of(k)] + b[:, strip_of(k)]

    over = [
        remote(a.at[yy * 2 + 1 - x], d.at[yy], d_send.at[yy], d_recv.at[yy], tok=xn) for yy in range(2)
    ]
    for o in over:
        o.start()
    for o in over:
        o.wait()
    sent[2].start()

    @pl.loop(0, CHUNKS)
    def _(k):
        for yy in range(2):
            e[yy, strip_of(k)] = a[yy * 2 + x, strip_of(k)] + d[yy, strip_of(k)]

    def rise(k):
        return remote(pout.at[:, strip_of(k)], pin.at[:, strip_of(k)], p_send.at[k], p_recv.at[k], ffn=above)

    def fall(k):
        return remote(qout.at[:, strip_of(k)], qin.at[:, strip_of(k)], q_send.at[k], q_recv.at[k], ffn=below)

    def line(first, last):
        for step in range(first, last):
            k = step - z

            @pl.when((k >= 0) & (k < CHUNKS))
            def _():
                @pl.when(z == 0)
                def _():
                    pout[:, strip_of(k)] = e[:, strip_of(k)]

                @pl.when(has_down)
                def _():
                    rise(k).wait_recv()
                    pout[:, strip_of(k)] = e[:, strip_of(k)] + pin[:, strip_of(k)]

                @pl.when(has_up)
                def _():
                    rise(k).start()

            n = step - (chips - 1 - z)

            @pl.when((n >= 0) & (n < CHUNKS))
            def _():
                @pl.when(z == chips - 1)
                def _():
                    qout[:, strip_of(n)] = e[:, strip_of(n)]

                @pl.when(has_up)
                def _():
                    fall(n).wait_recv()
                    qout[:, strip_of(n)] = e[:, strip_of(n)] + qin[:, strip_of(n)]

                @pl.when(has_down)
                def _():
                    fall(n).start()

    line(0, 2)
    via_x = part(y, 1 - x, 0)
    copy(via_x, y, 1 - x, 0, 0, xn).wait_recv()
    fy = copy(via_x, y, 1 - x, 0, 4, yn)
    fy.start()
    line(2, 4)
    via_y = part(1 - y, x, 1)
    copy(via_y, 1 - y, x, 1, 2, yn).wait_recv()
    fx = copy(via_y, 1 - y, x, 1, 5, xn)
    fx.start()
    line(4, CHUNKS + chips - 1)

    @pl.loop(0, CHUNKS)
    def _(k):
        @pl.when(has_up)
        def _():
            e[:, strip_of(k)] = pout[:, strip_of(k)] + qin[:, strip_of(k)]

        @pl.when(z == chips - 1)
        def _():
            e[:, strip_of(k)] = pout[:, strip_of(k)]

    def slab_rows(yy):
        return r_ref.at[pl.ds(pl.multiple_of(yy * rows + c * cut, 16), cut)]

    to_y = remote(e.at[1 - y], slab_rows(y), r_send.at[0], r_recv.at[0], tok=yn)
    to_y.start()
    to_core = remote(e.at[y], slab_rows(y), r_send.at[1], r_recv.at[1], ffn=partner)
    to_core.start()
    keep = pltpu.make_async_copy(e.at[y], slab_rows(y), l_sem.at[2])
    keep.start()
    from_y = slab_rows(1 - y)
    remote(e.at[1 - y], from_y, r_send.at[0], r_recv.at[0], tok=yn).wait_recv()
    again = remote(from_y, from_y, r_send.at[2], r_recv.at[2], ffn=partner)
    again.start()
    to_y.wait_send()
    to_core.wait()
    keep.wait()
    again.wait()

    @pl.loop(0, CHUNKS)
    def _(k):
        @pl.when(has_up)
        def _():
            rise(k).wait_send()

        @pl.when(has_down)
        def _():
            fall(k).wait_send()

    sent[2].wait_recv()
    sent[3].wait_recv()
    fy.wait()
    fx.wait()
    for s in sent:
        s.wait_send()
    local.wait()


def hidden_kernel(per, rows_ref, begin_ref, t_ref, g_ref, u_ref, h_ref, s_ref):
    i = pl.program_id(0)
    depth, width = g_ref.shape
    many = width // BLOCK
    wide = s_ref.shape[2] // BLOCK

    @pl.when(i == 0)
    def _():
        s_ref[...] = jnp.zeros_like(s_ref)

    for n in range(many):
        column = i * many + n
        span = pl.ds(n * BLOCK, BLOCK)
        tiles = []
        for k in range(depth // BLOCK):
            r = rows_ref[column, k]
            tile = t_ref[r // per, :, :, pl.ds(pl.multiple_of((r % per) * BLOCK, BLOCK), BLOCK)]
            tiles.append(tile.reshape(-1, BLOCK))
        picked = jnp.concatenate(tiles, axis=1)
        weights = jnp.concatenate([g_ref[:, span], u_ref[:, span]], axis=1)
        both = jnp.dot(picked, weights, preferred_element_type=jnp.float32)
        gate, up = both[:, :BLOCK], both[:, BLOCK:]
        hidden = (gate / (1.0 + jnp.exp(-gate)) * up).astype(h_ref.dtype)
        h_ref[:, span] = hidden
        at = column - begin_ref[0]

        @pl.when((at >= 0) & (at < wide * s_ref.shape[0]))
        def _():
            s_ref[at // wide, :, pl.ds(pl.multiple_of((at % wide) * BLOCK, BLOCK), BLOCK)] = hidden


def product_kernel(scale, a_ref, b_ref, o_ref, turned):
    @pl.when(pl.program_id(0) == 0)
    def _():
        turned[...] = a_ref[...].T

    o_ref[...] = jnp.dot(turned[...], b_ref[...], preferred_element_type=jnp.float32) * scale


def params(**more):
    return pltpu.CompilerParams(**more)


def shards_split(ffn, tokens, gate_blocks, up_blocks, block_rows, slab_offset):
    rows, feats = tokens.shape
    depth, panel = gate_blocks.shape
    half = panel // 2
    chips = ffn // 2
    bf = jnp.bfloat16
    dma = pltpu.SemaphoreType.DMA
    shape = jax.ShapeDtypeStruct
    spread_tokens, gates, ups = pl.pallas_call(
        functools.partial(spread, chips),
        out_shape=(shape((ffn, 2, rows, feats), bf), shape((4, depth, half), bf), shape((4, depth, half), bf)),
        in_specs=[ANY] * 3,
        out_specs=(ANY,) * 3,
        scratch_shapes=[
            dma((3, 2)), dma((3, 2)), dma((3,)), dma, dma,
            dma((chips, 2)), dma((chips, 2)), dma((chips, 2)),
            dma((chips, 2)), dma((chips, 2)), dma((chips, 2)),
        ],
        compiler_params=params(collective_id=0, has_side_effects=True),
        name="spread",
    )(tokens, gate_blocks, up_blocks)
    t = lax.axis_index("tok")
    f = lax.axis_index("ffn")
    count = half // BLOCK
    rows_here = lax.dynamic_slice_in_dim(block_rows, (t % 2) * count, count, 0)
    many = 2 if count % 2 == 0 else 1
    wide = SLAB // 4
    begin = slab_offset // BLOCK - (f * 2 + t % 2) * count
    hidden, slab = pl.pallas_call(
        functools.partial(hidden_kernel, feats // BLOCK),
        out_shape=(shape((2 * rows, half), bf), shape((4, 2 * rows, wide), bf)),
        grid_spec=pltpu.PrefetchScalarGridSpec(
            num_scalar_prefetch=2,
            grid=(count // many,),
            in_specs=[
                pl.BlockSpec(memory_space=pltpu.VMEM),
                pl.BlockSpec((4 * depth, many * BLOCK), lambda i, r, b: (0, i)),
                pl.BlockSpec((4 * depth, many * BLOCK), lambda i, r, b: (0, i)),
            ],
            out_specs=(
                pl.BlockSpec((2 * rows, many * BLOCK), lambda i, r, b: (0, i)),
                pl.BlockSpec((4, 2 * rows, wide), lambda i, r, b: (0, 0, 0)),
            ),
        ),
        compiler_params=params(vmem_limit_bytes=48 * 1024 * 1024),
        name="hidden",
    )(rows_here, begin, spread_tokens, gates.reshape(4 * depth, half), ups.reshape(4 * depth, half))
    vmem = pltpu.VMEM
    whole, row_panel = pl.pallas_call(
        functools.partial(join, chips),
        out_shape=(shape((4 * rows, panel), bf), shape((4 * rows, wide), bf)),
        in_specs=[ANY] * 2,
        out_specs=(ANY,) * 2,
        scratch_shapes=[
            vmem((4, rows, wide), bf), vmem((4, rows, wide), bf),
            *[vmem((2, rows, wide), bf) for _ in range(6)],
            dma((3,)), dma((6,)), dma((6,)), dma((2,)), dma((2,)), dma((2,)),
            *[dma((CHUNKS,)) for _ in range(4)],
            dma((3,)), dma((3,)),
        ],
        compiler_params=params(
            collective_id=1, has_side_effects=True, vmem_limit_bytes=32 * 1024 * 1024
        ),
        name="join",
    )(hidden, slab)
    tile = 512 if panel % 512 == 0 else BLOCK
    return pl.pallas_call(
        functools.partial(product_kernel, 2.0 / (4 * rows)),
        out_shape=shape((wide, panel), jnp.float32),
        grid=(panel // tile,),
        in_specs=[
            pl.BlockSpec((4 * rows, wide), lambda i: (0, 0)),
            pl.BlockSpec((4 * rows, tile), lambda i: (0, i)),
        ],
        out_specs=pl.BlockSpec((wide, tile), lambda i: (0, i)),
        scratch_shapes=[vmem((wide, 4 * rows), bf)],
        compiler_params=params(vmem_limit_bytes=48 * 1024 * 1024),
        name="product",
    )(row_panel, whole)


def shards(tokens, gate_blocks, up_blocks, block_rows, slab_offset):
    rows_here = tokens.shape[0]
    column_count = block_rows.shape[0]
    whole = lax.all_gather(tokens, "ffn", axis=1, tiled=True)
    feature_tiles = whole.reshape(rows_here, -1, BLOCK)
    chosen_entries = jnp.take(feature_tiles, block_rows, axis=1)
    pieces = (
        lax.all_gather(gate_blocks, "tok", axis=0, tiled=True),
        lax.all_gather(up_blocks, "tok", axis=0, tiled=True),
    )
    block_count = pieces[0].shape[0] // BLOCK
    gate_segment = pieces[0].reshape(block_count, BLOCK, column_count, BLOCK)
    up_segment = pieces[1].reshape(block_count, BLOCK, column_count, BLOCK)
    gate_add = jnp.einsum(
        "aqdh,dhqz->aqz", chosen_entries, gate_segment, preferred_element_type=jnp.float32
    )
    up_increment = jnp.einsum(
        "aqdh,dhqz->aqz", chosen_entries, up_segment, preferred_element_type=jnp.float32
    )
    panel_width = column_count * BLOCK
    hidden = (
        (jax.nn.silu(gate_add) * up_increment).astype(jnp.bfloat16).reshape(rows_here, panel_width)
    )
    column_panel = lax.all_gather(hidden, "tok", axis=0, tiled=True)
    ffn_place = lax.axis_index("ffn")
    begin_col = slab_offset[0] - ffn_place * panel_width
    padded = jnp.pad(hidden, ((0, 0), (SLAB, SLAB)))
    leading_column = jnp.clip(begin_col + SLAB, 0, panel_width + SLAB)
    slab_piece = lax.dynamic_slice_in_dim(padded, leading_column, SLAB, 1).astype(jnp.float32)
    summed = lax.psum(slab_piece.astype(jnp.bfloat16), "ffn")
    row_panel = lax.all_to_all(summed, "tok", split_axis=1, concat_axis=0, tiled=True)
    product = lax.dot_general(
        row_panel, column_panel, (((0,), (0,)), ((), ())), preferred_element_type=jnp.float32
    )
    return product * (2.0 / column_panel.shape[0])


def solution(mesh):
    ffn, tok = mesh.shape["ffn"], mesh.shape["tok"]

    def body(tokens, gate_blocks, up_blocks, block_rows, slab_offset):
        if tok == 4 and ffn >= 6 and ffn % 2 == 0 and block_rows.shape[0] % 2 == 0:
            return shards_split(ffn, tokens, gate_blocks, up_blocks, block_rows, slab_offset)
        return shards(tokens, gate_blocks, up_blocks, block_rows, slab_offset)

    in_specs = (
        P(("grp", "tok"), "ffn"),
        P(("grp", "tok"), "ffn"),
        P(("grp", "tok"), "ffn"),
        P(("grp", "ffn"), None),
        P("grp"),
    )
    out_specs = P(("grp", "tok"), "ffn")
    return jax.shard_map(body, mesh=mesh, in_specs=in_specs, out_specs=out_specs, check_vma=False)
```

```python
import functools

import jax
import jax.numpy as jnp
from jax import lax
from jax.experimental import pallas as pl
from jax.experimental.pallas import tpu as pltpu
from jax.sharding import PartitionSpec as P

BLOCK = 128
SLAB = 4096
MESH = pl.DeviceIdType.MESH
ANY = pl.BlockSpec(memory_space=pl.ANY)


def remote(src, dst, send, recv, **where):
    return pltpu.make_async_remote_copy(
        src_ref=src, dst_ref=dst, send_sem=send, recv_sem=recv, device_id=where, device_id_type=MESH
    )


def greet(others, z_there):
    barrier = pltpu.get_barrier_semaphore()
    for where in others:
        pl.semaphore_signal(barrier, inc=1, device_id=where, device_id_type=MESH)
    for there, where in z_there:
        @pl.when(there)
        def _():
            pl.semaphore_signal(barrier, inc=1, device_id=where, device_id_type=MESH)
    count = len(others)
    for there, _ in z_there:
        count = count + jnp.where(there, 1, 0)
    pl.semaphore_wait(barrier, count)


def places():
    f, t = lax.axis_index("ffn"), lax.axis_index("tok")
    z, c = f // 2, f % 2
    y, x = t // 2, t % 2
    return f, t, z, c, y, x


def spread(chips, tok_ref, gate_ref, up_ref, t_ref, g_ref, u_ref,
           w_send, w_recv, l_sem, x_send, x_recv, c_send, c_recv, up_send, up_recv, dn_send, dn_recv):
    f, t, z, c, y, x = places()
    half = g_ref.shape[2]
    xn, yn = y * 2 + 1 - x, (1 - y) * 2 + x
    partner = z * 2 + 1 - c
    above, below = f + 2, f - 2
    greet(
        [dict(tok=xn), dict(tok=yn), dict(ffn=partner)],
        [(z < chips - 1, dict(ffn=above)), (z > 0, dict(ffn=below))],
    )
    ends = []
    own = t_ref.at[f, x]
    cx = remote(tok_ref, own, x_send, x_recv, tok=xn)
    cx.start()

    def up(src, dst, zs, j):
        return remote(src, dst, up_send.at[zs, j], up_recv.at[zs, j], ffn=above)

    def down(src, dst, zs, j):
        return remote(src, dst, dn_send.at[zs, j], dn_recv.at[zs, j], ffn=below)

    def across(src, dst, zs, j):
        return remote(src, dst, c_send.at[zs, j], c_recv.at[zs, j], ffn=partner)

    def pass_on(src, dst, zs, j, go_up, go_down):
        if go_up is not None:
            @pl.when(go_up)
            def _():
                up(src, dst, zs, j).start()
        if go_down is not None:
            @pl.when(go_down)
            def _():
                down(src, dst, zs, j).start()
        across(src, dst, zs, j).start()

    pass_on(tok_ref, own, z, 0, z < chips - 1, z > 0)
    here = pl.ds(pl.multiple_of(x * half, BLOCK), half)
    there = pl.ds(pl.multiple_of((1 - x) * half, BLOCK), half)
    pairs = ((gate_ref, g_ref), (up_ref, u_ref))
    over_y = [remote(s.at[:, here], d.at[t], w_send.at[0, m], w_recv.at[0, m], tok=yn) for m, (s, d) in enumerate(pairs)]
    over_x = [remote(s.at[:, there], d.at[t], w_send.at[1, m], w_recv.at[1, m], tok=xn) for m, (s, d) in enumerate(pairs)]
    onward = [remote(d.at[xn], d.at[xn], w_send.at[2, m], w_recv.at[2, m], tok=yn) for m, (s, d) in enumerate(pairs)]
    for copy in over_y:
        copy.start()
    locals_ = [
        pltpu.make_async_copy(tok_ref, own, l_sem.at[0]),
        pltpu.make_async_copy(gate_ref.at[:, here], g_ref.at[t], l_sem.at[1]),
        pltpu.make_async_copy(up_ref.at[:, here], u_ref.at[t], l_sem.at[2]),
    ]
    for copy in locals_:
        copy.start()
    other = t_ref.at[f, 1 - x]
    remote(tok_ref, other, x_send, x_recv, tok=xn).wait_recv()
    pass_on(other, other, z, 1, z < chips - 1, z > 0)
    over_x[0].start()
    for k in range(1, chips):
        for j in range(2):
            xs = x if j == 0 else 1 - x

            @pl.when(z >= k)
            def _():
                piece = t_ref.at[f - 2 * k, xs]
                up(piece, piece, z - k, j).wait_recv()
                pass_on(piece, piece, z - k, j, z < chips - 1, None)

            @pl.when(z + k < chips)
            def _():
                piece = t_ref.at[f + 2 * k, xs]
                down(piece, piece, z + k, j).wait_recv()
                pass_on(piece, piece, z + k, j, None, z > 0)

        if k < 3:
            over_x[k - 1].wait_recv()
            onward[k - 1].start()
            if k == 1:
                over_x[0].wait_send()
                over_x[1].start()

    for zs in range(chips):
        for j in range(2):
            xs = x if j == 0 else 1 - x
            got = t_ref.at[zs * 2 + 1 - c, xs]
            across(got, got, zs, j).wait_recv()
            across(got, got, zs, j).wait_send()

            @pl.when((zs <= z) & (z < chips - 1))
            def _():
                up(got, got, zs, j).wait_send()

            @pl.when((zs >= z) & (z > 0))
            def _():
                down(got, got, zs, j).wait_send()

    cx.wait_send()
    for copy in locals_:
        copy.wait()
    for copy in over_y + onward:
        copy.wait()
    over_x[1].wait_send()


CHUNKS = 4


def join(chips, h_ref, s_ref, p_ref, r_ref, a, b, d, e, pin, qin, pout, qout,
         l_sem, send, recv, b_sem, d_send, d_recv, p_send, p_recv, q_send, q_recv, r_send, r_recv):
    f, t, z, c, y, x = places()
    rows, half = h_ref.shape
    xn, yn = y * 2 + 1 - x, (1 - y) * 2 + x
    partner = z * 2 + 1 - c
    above, below = f + 2, f - 2
    has_up, has_down = z < chips - 1, z > 0
    greet(
        [dict(tok=xn), dict(tok=yn), dict(ffn=partner)],
        [(has_up, dict(ffn=above)), (has_down, dict(ffn=below))],
    )
    cut = rows // 2

    first = rows * 9 // 16
    spans = ((0, first), (first, rows - first))

    def part(yy, xx, s):
        return p_ref.at[
            pl.ds(pl.multiple_of(yy * rows + spans[s][0], 16), spans[s][1]),
            pl.ds(pl.multiple_of(xx * half, BLOCK), half),
        ]

    def copy(src, yy, xx, s, n, there):
        return remote(src, part(yy, xx, s), send.at[n], recv.at[n], tok=there)

    own = [h_ref.at[pl.ds(*span)] for span in spans]
    sent = [
        copy(own[0], y, x, 0, 0, xn), copy(own[1], y, x, 1, 2, yn),
        copy(own[1], y, x, 1, 1, xn), copy(own[0], y, x, 0, 3, yn),
    ]
    mine, theirs = (pl.ds(pl.multiple_of(k * cut, 16), cut) for k in (c, 1 - c))
    swap = remote(s_ref.at[:, theirs], b, b_sem.at[0], b_sem.at[1], ffn=partner)
    swap.start()
    load = pltpu.make_async_copy(s_ref.at[:, mine], a, l_sem.at[1])
    load.start()
    sent[0].start()
    sent[1].start()
    sent[3].start()
    local = pltpu.make_async_copy(
        h_ref,
        p_ref.at[pl.ds(pl.multiple_of(y * rows, 16), rows), pl.ds(pl.multiple_of(x * half, BLOCK), half)],
        l_sem.at[0],
    )
    local.start()
    load.wait()
    swap.wait()

    strip = cut // CHUNKS

    def strip_of(k):
        return pl.ds(pl.multiple_of(k * strip, 16), strip)

    @pl.loop(0, CHUNKS)
    def _(k):
        a[:, strip_of(k)] = a[:, strip_of(k)] + b[:, strip_of(k)]

    over = [
        remote(a.at[yy * 2 + 1 - x], d.at[yy], d_send.at[yy], d_recv.at[yy], tok=xn) for yy in range(2)
    ]
    for o in over:
        o.start()
    for o in over:
        o.wait()
    sent[2].start()

    @pl.loop(0, CHUNKS)
    def _(k):
        for yy in range(2):
            e[yy, strip_of(k)] = a[yy * 2 + x, strip_of(k)] + d[yy, strip_of(k)]

    def rise(k):
        return remote(pout.at[:, strip_of(k)], pin.at[:, strip_of(k)], p_send.at[k], p_recv.at[k], ffn=above)

    def fall(k):
        return remote(qout.at[:, strip_of(k)], qin.at[:, strip_of(k)], q_send.at[k], q_recv.at[k], ffn=below)

    def line(first, last):
        for step in range(first, last):
            k = step - z

            @pl.when((k >= 0) & (k < CHUNKS))
            def _():
                @pl.when(z == 0)
                def _():
                    pout[:, strip_of(k)] = e[:, strip_of(k)]

                @pl.when(has_down)
                def _():
                    rise(k).wait_recv()
                    pout[:, strip_of(k)] = e[:, strip_of(k)] + pin[:, strip_of(k)]

                @pl.when(has_up)
                def _():
                    rise(k).start()

            n = step - (chips - 1 - z)

            @pl.when((n >= 0) & (n < CHUNKS))
            def _():
                @pl.when(z == chips - 1)
                def _():
                    qout[:, strip_of(n)] = e[:, strip_of(n)]

                @pl.when(has_up)
                def _():
                    fall(n).wait_recv()
                    qout[:, strip_of(n)] = e[:, strip_of(n)] + qin[:, strip_of(n)]

                @pl.when(has_down)
                def _():
                    fall(n).start()

    line(0, 2)
    via_x = part(y, 1 - x, 0)
    copy(via_x, y, 1 - x, 0, 0, xn).wait_recv()
    fy = copy(via_x, y, 1 - x, 0, 4, yn)
    fy.start()
    line(2, 4)
    via_y = part(1 - y, x, 1)
    copy(via_y, 1 - y, x, 1, 2, yn).wait_recv()
    fx = copy(via_y, 1 - y, x, 1, 5, xn)
    fx.start()
    line(4, CHUNKS + chips - 1)

    @pl.loop(0, CHUNKS)
    def _(k):
        @pl.when(has_up)
        def _():
            e[:, strip_of(k)] = pout[:, strip_of(k)] + qin[:, strip_of(k)]

        @pl.when(z == chips - 1)
        def _():
            e[:, strip_of(k)] = pout[:, strip_of(k)]

    def slab_rows(yy):
        return r_ref.at[pl.ds(pl.multiple_of(yy * rows + c * cut, 16), cut)]

    to_y = remote(e.at[1 - y], slab_rows(y), r_send.at[0], r_recv.at[0], tok=yn)
    to_y.start()
    to_core = remote(e.at[y], slab_rows(y), r_send.at[1], r_recv.at[1], ffn=partner)
    to_core.start()
    keep = pltpu.make_async_copy(e.at[y], slab_rows(y), l_sem.at[2])
    keep.start()
    from_y = slab_rows(1 - y)
    remote(e.at[1 - y], from_y, r_send.at[0], r_recv.at[0], tok=yn).wait_recv()
    again = remote(from_y, from_y, r_send.at[2], r_recv.at[2], ffn=partner)
    again.start()
    to_y.wait_send()
    to_core.wait()
    keep.wait()
    again.wait()

    @pl.loop(0, CHUNKS)
    def _(k):
        @pl.when(has_up)
        def _():
            rise(k).wait_send()

        @pl.when(has_down)
        def _():
            fall(k).wait_send()

    sent[2].wait_recv()
    sent[3].wait_recv()
    fy.wait()
    fx.wait()
    for s in sent:
        s.wait_send()
    local.wait()


def hidden_kernel(per, rows_ref, begin_ref, t_ref, g_ref, u_ref, h_ref, s_ref):
    i = pl.program_id(0)
    depth, width = g_ref.shape
    many = width // BLOCK
    wide = s_ref.shape[2] // BLOCK

    @pl.when(i == 0)
    def _():
        s_ref[...] = jnp.zeros_like(s_ref)

    for n in range(many):
        column = i * many + n
        span = pl.ds(n * BLOCK, BLOCK)
        tiles = []
        for k in range(depth // BLOCK):
            r = rows_ref[column, k]
            tile = t_ref[r // per, :, :, pl.ds(pl.multiple_of((r % per) * BLOCK, BLOCK), BLOCK)]
            tiles.append(tile.reshape(-1, BLOCK))
        picked = jnp.concatenate(tiles, axis=1)
        weights = jnp.concatenate([g_ref[:, span], u_ref[:, span]], axis=1)
        both = jnp.dot(picked, weights, preferred_element_type=jnp.float32)
        gate, up = both[:, :BLOCK], both[:, BLOCK:]
        hidden = (gate / (1.0 + jnp.exp(-gate)) * up).astype(h_ref.dtype)
        h_ref[:, span] = hidden
        at = column - begin_ref[0]

        @pl.when((at >= 0) & (at < wide * s_ref.shape[0]))
        def _():
            s_ref[at // wide, :, pl.ds(pl.multiple_of((at % wide) * BLOCK, BLOCK), BLOCK)] = hidden


def product_kernel(scale, a_ref, b_ref, o_ref, turned):
    @pl.when(pl.program_id(0) == 0)
    def _():
        turned[...] = a_ref[...].T

    o_ref[...] = jnp.dot(turned[...], b_ref[...], preferred_element_type=jnp.float32) * scale


def params(**more):
    return pltpu.CompilerParams(**more)


def shards_split(ffn, tokens, gate_blocks, up_blocks, block_rows, slab_offset):
    rows, feats = tokens.shape
    depth, panel = gate_blocks.shape
    half = panel // 2
    chips = ffn // 2
    bf = jnp.bfloat16
    dma = pltpu.SemaphoreType.DMA
    shape = jax.ShapeDtypeStruct
    spread_tokens, gates, ups = pl.pallas_call(
        functools.partial(spread, chips),
        out_shape=(shape((ffn, 2, rows, feats), bf), shape((4, depth, half), bf), shape((4, depth, half), bf)),
        in_specs=[ANY] * 3,
        out_specs=(ANY,) * 3,
        scratch_shapes=[
            dma((3, 2)), dma((3, 2)), dma((3,)), dma, dma,
            dma((chips, 2)), dma((chips, 2)), dma((chips, 2)),
            dma((chips, 2)), dma((chips, 2)), dma((chips, 2)),
        ],
        compiler_params=params(collective_id=0, has_side_effects=True),
        name="spread",
    )(tokens, gate_blocks, up_blocks)
    t = lax.axis_index("tok")
    f = lax.axis_index("ffn")
    count = half // BLOCK
    rows_here = lax.dynamic_slice_in_dim(block_rows, (t % 2) * count, count, 0)
    many = 2 if count % 2 == 0 else 1
    wide = SLAB // 4
    begin = slab_offset // BLOCK - (f * 2 + t % 2) * count
    hidden, slab = pl.pallas_call(
        functools.partial(hidden_kernel, feats // BLOCK),
        out_shape=(shape((2 * rows, half), bf), shape((4, 2 * rows, wide), bf)),
        grid_spec=pltpu.PrefetchScalarGridSpec(
            num_scalar_prefetch=2,
            grid=(count // many,),
            in_specs=[
                pl.BlockSpec(memory_space=pltpu.VMEM),
                pl.BlockSpec((4 * depth, many * BLOCK), lambda i, r, b: (0, i)),
                pl.BlockSpec((4 * depth, many * BLOCK), lambda i, r, b: (0, i)),
            ],
            out_specs=(
                pl.BlockSpec((2 * rows, many * BLOCK), lambda i, r, b: (0, i)),
                pl.BlockSpec((4, 2 * rows, wide), lambda i, r, b: (0, 0, 0)),
            ),
        ),
        compiler_params=params(vmem_limit_bytes=60 * 1024 * 1024),
        name="hidden",
    )(rows_here, begin, spread_tokens, gates.reshape(4 * depth, half), ups.reshape(4 * depth, half))
    vmem = pltpu.VMEM
    whole, row_panel = pl.pallas_call(
        functools.partial(join, chips),
        out_shape=(shape((4 * rows, panel), bf), shape((4 * rows, wide), bf)),
        in_specs=[ANY] * 2,
        out_specs=(ANY,) * 2,
        scratch_shapes=[
            vmem((4, rows, wide), bf), vmem((4, rows, wide), bf),
            *[vmem((2, rows, wide), bf) for _ in range(6)],
            dma((3,)), dma((6,)), dma((6,)), dma((2,)), dma((2,)), dma((2,)),
            *[dma((CHUNKS,)) for _ in range(4)],
            dma((3,)), dma((3,)),
        ],
        compiler_params=params(
            collective_id=1, has_side_effects=True, vmem_limit_bytes=60 * 1024 * 1024
        ),
        name="join",
    )(hidden, slab)
    tile = 512 if panel % 512 == 0 else BLOCK
    return pl.pallas_call(
        functools.partial(product_kernel, 2.0 / (4 * rows)),
        out_shape=shape((wide, panel), jnp.float32),
        grid=(panel // tile,),
        in_specs=[
            pl.BlockSpec((4 * rows, wide), lambda i: (0, 0)),
            pl.BlockSpec((4 * rows, tile), lambda i: (0, i)),
        ],
        out_specs=pl.BlockSpec((wide, tile), lambda i: (0, i)),
        scratch_shapes=[vmem((wide, 4 * rows), bf)],
        compiler_params=params(vmem_limit_bytes=60 * 1024 * 1024),
        name="product",
    )(row_panel, whole)


def shards(tokens, gate_blocks, up_blocks, block_rows, slab_offset):
    rows_here = tokens.shape[0]
    column_count = block_rows.shape[0]
    whole = lax.all_gather(tokens, "ffn", axis=1, tiled=True)
    feature_tiles = whole.reshape(rows_here, -1, BLOCK)
    chosen_entries = jnp.take(feature_tiles, block_rows, axis=1)
    pieces = (
        lax.all_gather(gate_blocks, "tok", axis=0, tiled=True),
        lax.all_gather(up_blocks, "tok", axis=0, tiled=True),
    )
    block_count = pieces[0].shape[0] // BLOCK
    gate_segment = pieces[0].reshape(block_count, BLOCK, column_count, BLOCK)
    up_segment = pieces[1].reshape(block_count, BLOCK, column_count, BLOCK)
    gate_add = jnp.einsum(
        "aqdh,dhqz->aqz", chosen_entries, gate_segment, preferred_element_type=jnp.float32
    )
    up_increment = jnp.einsum(
        "aqdh,dhqz->aqz", chosen_entries, up_segment, preferred_element_type=jnp.float32
    )
    panel_width = column_count * BLOCK
    hidden = (
        (jax.nn.silu(gate_add) * up_increment).astype(jnp.bfloat16).reshape(rows_here, panel_width)
    )
    column_panel = lax.all_gather(hidden, "tok", axis=0, tiled=True)
    ffn_place = lax.axis_index("ffn")
    begin_col = slab_offset[0] - ffn_place * panel_width
    padded = jnp.pad(hidden, ((0, 0), (SLAB, SLAB)))
    leading_column = jnp.clip(begin_col + SLAB, 0, panel_width + SLAB)
    slab_piece = lax.dynamic_slice_in_dim(padded, leading_column, SLAB, 1).astype(jnp.float32)
    summed = lax.psum(slab_piece.astype(jnp.bfloat16), "ffn")
    row_panel = lax.all_to_all(summed, "tok", split_axis=1, concat_axis=0, tiled=True)
    product = lax.dot_general(
        row_panel, column_panel, (((0,), (0,)), ((), ())), preferred_element_type=jnp.float32
    )
    return product * (2.0 / column_panel.shape[0])


def solution(mesh):
    ffn, tok = mesh.shape["ffn"], mesh.shape["tok"]

    def body(tokens, gate_blocks, up_blocks, block_rows, slab_offset):
        if tok == 4 and ffn >= 6 and ffn % 2 == 0 and block_rows.shape[0] % 2 == 0:
            return shards_split(ffn, tokens, gate_blocks, up_blocks, block_rows, slab_offset)
        return shards(tokens, gate_blocks, up_blocks, block_rows, slab_offset)

    in_specs = (
        P(("grp", "tok"), "ffn"),
        P(("grp", "tok"), "ffn"),
        P(("grp", "tok"), "ffn"),
        P(("grp", "ffn"), None),
        P("grp"),
    )
    out_specs = P(("grp", "tok"), "ffn")
    return jax.shard_map(body, mesh=mesh, in_specs=in_specs, out_specs=out_specs, check_vma=False)
```
